128 devices in a mesh: theta: 16 (over z, x_hi, core), ax: 8 (over x_lo, y).
Axes of the slice: x: 4 (x_hi: 2, x_lo: 2; x = x_hi * 2 + x_lo), y: 4, z: 4, core: 2. Of those that a mesh axis runs over, the one named last changes fastest.
Arguments:
- state: float32 [5, 1024, 64, 1024], P(None, 'theta', None, 'ax'), as said below
- viscosity: float32 [1024, 64, 1024], P('theta', None, 'ax'), may hold values from 0.05 to 0.5
- band_rims: float32 [5, 1024, 4, 1024], P(None, 'theta', None, 'ax'), as said below
- coupling: float32 [5, 5], replicated, may hold values from -2.5 to 2.5
- block_map: int32 [8], replicated, may hold values from 0 to 7, as said below
- plane_flags: int32 [8], replicated, may hold values from 0 to 3
- mode_cutoff: int32 [1], replicated, may hold values from 2 to 256
Outputs:
- updated: float32 [5, 1024, 64, 1024], P(None, 'theta', None, 'ax')
The draws below stay inside these ranges and needn't reach their ends.
Inputs may be any that keep to these rules, and one draw needn't show every extreme that they name: `block_map`: entries of plane_flags; the values 0 and 7 both appear. `state`: density within 0.8 to 1.2, momenta within -1 to 1, energy within 2 to 3. `band_rims`: density within 0.8 to 1.2, momenta within -1 to 1, energy within 2 to 3.
All inputs are finite; a program needn't handle non-finite values.
Results may differ from the reference program's by a relative error of at most 0.0003.
Values sent between devices are 32-bit elements; how exact they have to be, the bound alone decides.
A program may use at most 640 MiB of HBM per device.

```python
import math
import jax
import jax.numpy as jnp
from jax import lax

CT = 64
CR = 64
CX = 128
NT = 1024
NX = 1024
N_THETA = 16
N_AX = 8


def conserved(key, extent, smallest, density_width, energy_width):
    subkeys = jax.random.split(key, 4)
    levels = jax.random.randint(subkeys[0], (2,) + extent, 0, 2).astype(jnp.float32)
    spread = jax.random.uniform(subkeys[1], (2,) + extent, jnp.float32, 0.0, 1.0)
    density = 0.8 + 0.4 * levels[0] + density_width * spread[0] * (1.0 - 2.0 * levels[0])
    energy = 2.0 + levels[1] + energy_width * spread[1] * (1.0 - 2.0 * levels[1])
    polarity = (2 * jax.random.randint(subkeys[2], (3,) + extent, 0, 2) - 1).astype(jnp.float32)
    magnitude = jax.random.uniform(subkeys[3], (3,) + extent, jnp.float32, smallest, 1.0)
    momentum = jnp.clip(polarity * magnitude, -1.0, 1.0)
    return jnp.concatenate([density[None], momentum, energy[None]], 0)


def draw_state(key, part):
    key = jax.random.fold_in(key, 11)
    extent = (NT, CR, NX)
    return conserved(key, extent, 0.75, 0.1, 0.25)


def draw_band_rims(key, part):
    key = jax.random.fold_in(key, 23)
    extent = (NT, 4, NX)
    return conserved(key, extent, 0.75, 0.1, 0.25)


def draw_block_map(key, part):
    key = jax.random.fold_in(key, 37)
    keys = jax.random.split(key, 3)
    ordered = jax.random.permutation(keys[0], jnp.arange(N_AX, dtype=jnp.int32))
    other = jax.random.randint(keys[1], (N_AX,), 0, N_AX, dtype=jnp.int32)
    coin = jax.random.randint(keys[2], (N_AX,), 0, 2, dtype=jnp.int32)
    keep = (coin == 1) | (ordered == 0) | (ordered == N_AX - 1)
    return jnp.where(keep, ordered, other).astype(jnp.int32)


def set_ends(array, own_key, least, largest):
    shape = array.shape
    index_at = [jax.random.randint(jax.random.fold_in(own_key, axis), (), 0, shape[axis]) for axis in range(len(shape))]
    array = array.at[tuple(index_at)].set(least)
    longest = shape.index(max(shape))
    index_at[longest] = (index_at[longest] + 1) % shape[longest]
    return array.at[tuple(index_at)].set(largest)


def level_of(stream_key, shape, shards, low, largest):
    def one(dim, parts):
        steps = jax.random.uniform(jax.random.fold_in(jax.random.fold_in(stream_key, 6), dim), (parts,), jnp.float32, low / len(shards), largest / len(shards))
        return jnp.repeat(jnp.exp(steps), shape[dim] // parts).reshape((-1,) + (1,) * (len(shape) - dim - 1))

    factor_of = one(*shards[0])
    for cut in shards[1:]:
        factor_of = factor_of * one(*cut)
    return factor_of


def scatter_about(stream_key, shape, deviation, limit, kind=jnp.bfloat16):
    values = jax.random.normal(stream_key, shape, jnp.float32) * deviation
    return jnp.minimum(jnp.maximum(values, -limit), limit).astype(kind)


def setup_inputs(seed: int = 0) -> dict:
    key_of = jax.random.split(jax.random.key(seed), 8)
    state = draw_state(jax.random.fold_in(key_of[7], 71), 0)
    viscosity = jnp.clip(jnp.exp(math.log(0.5) - 2.3025851 * jax.random.uniform(key_of[1], (NT, CR, NX), jnp.float32) ** level_of(key_of[1], (NT, CR, NX), ((0, 16), (2, 8)), -0.2, 0.2)), 0.05, 0.5)
    band_rims = draw_band_rims(jax.random.fold_in(key_of[7], 71), 0)
    coupling = scatter_about(key_of[3], (5, 5), 0.4, 2.5, jnp.float32)
    block_map = draw_block_map(jax.random.fold_in(key_of[7], 71), 0)
    plane_flags = set_ends(jax.random.randint(key_of[5], (N_AX,), 0, 4), jax.random.fold_in(key_of[5], 1), 0, 3).astype(jnp.int32)
    mode_cutoff = jax.random.randint(key_of[6], (1,), 2, NT // 4 + 1).astype(jnp.int32)
    return dict(state=state, viscosity=viscosity, band_rims=band_rims, coupling=coupling, block_map=block_map, plane_flags=plane_flags, mode_cutoff=mode_cutoff)


section_step = 0.2


def primitive_fluxes(field):
    density = field[0]
    inverse = 1.0 / density
    axial_vel = field[1] * inverse
    radial_vel = field[2] * inverse
    swirl_vel = field[3] * inverse
    pressure = 0.4 * (field[4] - 0.5 * (field[1] * axial_vel + field[2] * radial_vel + field[3] * swirl_vel))
    enthalpy = field[4] + pressure
    axial_flux = jnp.stack([field[1], field[1] * axial_vel + pressure, field[2] * axial_vel, field[3] * axial_vel, enthalpy * axial_vel])
    radial_flux = jnp.stack([field[2], field[1] * radial_vel, field[2] * radial_vel + pressure, field[3] * radial_vel, enthalpy * radial_vel])
    swirl_flux = jnp.stack([field[3], field[1] * swirl_vel, field[2] * swirl_vel, field[3] * swirl_vel + pressure, enthalpy * swirl_vel])
    return axial_flux, radial_flux, swirl_flux


def radial_pad(field, radial_flux, band_rims):
    rim_flux = primitive_fluxes(band_rims)[1]
    radial_padded = jnp.concatenate([rim_flux[:, :, :2], radial_flux, rim_flux[:, :, 2:]], 2)
    cells_radial = jnp.concatenate([band_rims[:, :, :2], field, band_rims[:, :, 2:]], 2)
    return radial_padded, cells_radial


def derivative(padded, axis, count):
    def part(offset):
        return lax.slice_in_dim(padded, offset, offset + count, axis=axis)
    return (8.0 * (part(3) - part(1)) - (part(4) - part(0))) / 12.0


def second_diff(padded, axis, count, field):
    return lax.slice_in_dim(padded, 1, 1 + count, axis=axis) + lax.slice_in_dim(padded, 3, 3 + count, axis=axis) - 2.0 * field


def section_update(field, axial_padded, swirl_padded, radial_padded, cells_axial, cells_swirl, cells_radial, viscosity):
    count_swirl = field.shape[1]
    count_radial = field.shape[2]
    count_axial = field.shape[3]
    divergence = derivative(axial_padded, 3, count_axial) + derivative(radial_padded, 2, count_radial) + derivative(swirl_padded, 1, count_swirl)
    laplacian = second_diff(cells_axial, 3, count_axial, field) + second_diff(cells_radial, 2, count_radial, field) + second_diff(cells_swirl, 1, count_swirl, field)
    return field + section_step * (viscosity[None] * laplacian - divergence)


def mode_tables(first, count, total):
    rows_here = first + jnp.arange(count, dtype=jnp.int32)
    modes = jnp.arange(total, dtype=jnp.int32)
    phase = (rows_here[:, None] * modes[None, :]) % total
    angle = (2.0 * math.pi / total) * phase.astype(jnp.float32)
    return jnp.cos(angle), jnp.sin(angle)


def mode_weights(mode_cutoff, total):
    modes = jnp.arange(total, dtype=jnp.int32)
    folded = jnp.minimum(modes, total - modes)
    return ((folded >= 1) & (folded < mode_cutoff[0])).astype(jnp.float32)


def giles_correct(planes, coupling, mode_cutoff):
    total = planes.shape[2]
    highest = lax.Precision.HIGHEST
    cosine, sine = mode_tables(0, total, total)
    weights = mode_weights(mode_cutoff, total)[:, None]
    real_part = jnp.einsum("kvtr,tm->kvmr", planes, cosine, precision=highest) * weights
    imag_part = jnp.einsum("kvtr,tm->kvmr", planes, sine, precision=highest) * weights
    filtered = (jnp.einsum("kvmr,tm->kvtr", real_part, cosine, precision=highest) + jnp.einsum("kvmr,tm->kvtr", imag_part, sine, precision=highest)) / total
    return planes + jnp.einsum("uv,kvtr->kutr", coupling, filtered, precision=highest)


def reference(state, viscosity, band_rims, coupling, block_map, plane_flags, mode_cutoff):
    total = state.shape[1]

    def sector_update(sector):
        rows_here = (sector * CT - 2 + jnp.arange(CT + 4, dtype=jnp.int32)) % total
        cells_swirl = jnp.take(state, rows_here, axis=1)
        axial_flux, radial_flux, swirl_flux = primitive_fluxes(cells_swirl)
        field = cells_swirl[:, 2:-2]
        widen = ((0, 0), (0, 0), (0, 0), (2, 2))
        axial_padded = jnp.pad(axial_flux[:, 2:-2], widen)
        cells_axial = jnp.pad(field, widen)
        local_visc = lax.dynamic_slice_in_dim(viscosity, (sector * CT).astype(jnp.int32), CT, 0)
        local_rims = lax.dynamic_slice_in_dim(band_rims, (sector * CT).astype(jnp.int32), CT, 1)
        radial_padded, cells_radial = radial_pad(field, radial_flux[:, 2:-2], local_rims)
        return section_update(field, axial_padded, swirl_flux, radial_padded, cells_axial, cells_swirl, cells_radial, local_visc)

    sectors = lax.map(sector_update, jnp.arange(N_THETA, dtype=jnp.int32))
    updated = jnp.moveaxis(sectors, 0, 1).reshape(state.shape)
    for block in range(N_AX):
        flag = plane_flags[block_map[block]]
        first = block * CX
        final = first + CX - 1
        planes = jnp.stack([updated[:, :, :, first], updated[:, :, :, final]])
        fixed = giles_correct(planes, coupling, mode_cutoff)
        updated = updated.at[:, :, :, first].set(jnp.where(flag % 2 == 1, fixed[0], planes[0]))
        updated = updated.at[:, :, :, final].set(jnp.where(flag // 2 == 1, fixed[1], planes[1]))
    return updated
```

```python
import functools
import math

import jax
import jax.numpy as jnp
import numpy as np
from jax import lax
from jax.experimental import pallas as pl
from jax.experimental.pallas import tpu as pltpu
from jax.sharding import PartitionSpec as P

UNIT = 0.2 / 12.0
V = 5
T = 64
R = 64
X = 128
TILE = 8
PAD = R + 2 * TILE
GROUPS = 4
PER = 16
CHUNK = 8
ROWS = 24
MESH = pl.DeviceIdType.MESH


def inverse_of(density):
    guess = pl.reciprocal(density, approx=True)
    return guess * (2.0 - density * guess)


def velocities(q):
    inv = inverse_of(q[0])
    u, v, w = q[1] * inv, q[2] * inv, q[3] * inv
    p = 0.4 * (q[4] - 0.5 * (q[1] * u + q[2] * v + q[3] * w))
    return u, v, w, p, q[4] + p


def flux_x(q, vel):
    u, v, w, p, h = vel
    return [q[1], q[1] * u + p, q[2] * u, q[3] * u, h * u]


def flux_r(q, vel):
    u, v, w, p, h = vel
    return [q[2], q[2] * u, q[2] * v + p, q[3] * v, h * v]


def flux_t(q, vel):
    u, v, w, p, h = vel
    return [q[3], q[3] * u, q[3] * v, q[3] * w + p, h * w]


def roll(x, shift):
    return pltpu.roll(x, shift % X, 1)


def lanes_of(rows=TILE):
    return lax.broadcasted_iota(jnp.int32, (rows, X), 1)


def section_body(
    state, visc, rims, sector, edges, out,
    q, nu, rim, edg, fr, ft, res, in_sem, misc_sem, out_sem,
):
    n_chunks = T // CHUNK

    def fetch(c):
        t0 = c * CHUNK
        return (
            pltpu.make_async_copy(
                state.at[:, pl.ds(t0, CHUNK)],
                q.at[:, pl.ds(t0 + 2, CHUNK), pl.ds(TILE, R)],
                in_sem.at[0, c],
            ),
            pltpu.make_async_copy(
                visc.at[pl.ds(t0, CHUNK)], nu.at[pl.ds(t0, CHUNK)], in_sem.at[1, c]
            ),
        )

    misc = [
        pltpu.make_async_copy(sector.at[0], q.at[:, pl.ds(0, 2), pl.ds(TILE, R)], misc_sem.at[0]),
        pltpu.make_async_copy(
            sector.at[1], q.at[:, pl.ds(T + 2, 2), pl.ds(TILE, R)], misc_sem.at[1]
        ),
        pltpu.make_async_copy(rims, rim, misc_sem.at[2]),
        pltpu.make_async_copy(edges, edg, misc_sem.at[3]),
    ]
    misc[0].start()
    for copy in fetch(0):
        copy.start()
    for copy in misc[1:]:
        copy.start()
    for c in range(1, n_chunks):
        for copy in fetch(c):
            copy.start()

    lane = lanes_of()
    edge_lanes = (lane < 2) | (lane >= X - 2)

    def circum_only(s):
        for k in range(R // TILE):
            rows = pl.ds(TILE + k * TILE, TILE)
            cell = [q[v, s, rows, :] for v in range(V)]
            f = flux_t(cell, velocities(cell))
            for v in range(1, V):
                ft[v - 1, s, pl.ds(k * TILE, TILE), :] = f[v]

    def first_half(s):
        t = s - 2
        for v in range(V):
            q[v, s, pl.ds(TILE - 2, 2), :] = rim[v, t, pl.ds(0, 2), :]
            q[v, s, pl.ds(TILE + R, 2), :] = rim[v, t, pl.ds(2, 2), :]
        cell = [rim[v, t, :, :] for v in range(V)]
        f = flux_r(cell, velocities(cell))
        for v in range(1, V):
            fr[v - 1, t, pl.ds(TILE - 2, 2), :] = f[v][0:2]
            fr[v - 1, t, pl.ds(TILE + R, 2), :] = f[v][2:4]
        for k in range(R // TILE):
            rows = pl.ds(k * TILE, TILE)
            wide = pl.ds(TILE + k * TILE, TILE)
            cell = [q[v, s, wide, :] for v in range(V)]
            vel = velocities(cell)
            f = flux_r(cell, vel)
            for v in range(1, V):
                fr[v - 1, t, wide, :] = f[v]
            f = flux_t(cell, vel)
            for v in range(1, V):
                ft[v - 1, s, rows, :] = f[v]
            f = flux_x(cell, vel)
            n = nu[t, rows, :]
            n12 = 12.0 * n
            kq = 60.0 - 72.0 * n
            for v in range(V):
                near = roll(f[v], -1) - roll(f[v], 1)
                far = roll(f[v], -2) - roll(f[v], 2)
                side = roll(cell[v], -1) + roll(cell[v], 1)
                res[v, t, rows, :] = kq * cell[v] + n12 * side - 8.0 * near + far

    def second_half(t):
        s = t + 2
        group = t // PER
        back = X - 4 + (-8 * (t % PER))
        back = lax.rem(back + X, X)
        for k in range(R // TILE):
            rows = pl.ds(k * TILE, TILE)
            base = TILE + k * TILE
            n12 = 12.0 * nu[t, rows, :]
            for v in range(V):

                def rad(o):
                    at = pl.ds(base + o, TILE)
                    return q[2, s, at, :] if v == 0 else fr[v - 1, t, at, :]

                def cir(o):
                    if v == 0:
                        return q[3, s + o, pl.ds(base, TILE), :]
                    return ft[v - 1, s + o, rows, :]

                near = (rad(1) - rad(-1)) + (cir(1) - cir(-1))
                far = (rad(2) - rad(-2)) + (cir(2) - cir(-2))
                side = (q[v, s, pl.ds(base + 1, TILE), :] + q[v, s, pl.ds(base - 1, TILE), :]) + (
                    q[v, s + 1, pl.ds(base, TILE), :] + q[v, s - 1, pl.ds(base, TILE), :]
                )
                got = UNIT * (res[v, t, rows, :] + n12 * side - 8.0 * near + far)
                edge = pltpu.roll(edg[group, v, rows, :], back, 1)
                res[v, t, rows, :] = jnp.where(edge_lanes, edge, got)

    def send(t0, count, c):
        return pltpu.make_async_copy(
            res.at[:, pl.ds(t0, count)], out.at[:, pl.ds(t0, count)], out_sem.at[c]
        )

    misc[0].wait()
    circum_only(0)
    circum_only(1)
    for copy in fetch(0):
        copy.wait()
    misc[2].wait()
    misc[3].wait()
    first_half(2)
    first_half(3)

    def steps(low, high):
        def step(s, carry):
            first_half(s)
            second_half(s - 4)
            return carry

        lax.fori_loop(low, high, step, 0)

    steps(4, CHUNK + 2)
    send(0, CHUNK - 2, 0).start()

    def chunk(c, carry):
        for copy in fetch(c):
            copy.wait()
        steps(c * CHUNK + 2, c * CHUNK + CHUNK + 2)
        send(c * CHUNK - 2, CHUNK, c).start()
        return carry

    lax.fori_loop(1, n_chunks, chunk, 0)
    misc[1].wait()
    circum_only(T + 2)
    circum_only(T + 3)
    second_half(T - 2)
    second_half(T - 1)
    send(T - 2, 2, n_chunks).start()
    send(0, CHUNK - 2, 0).wait()

    def drain(c, carry):
        send(c * CHUNK - 2, CHUNK, c).wait()
        return carry

    lax.fori_loop(1, n_chunks, drain, 0)
    send(T - 2, 2, n_chunks).wait()


def section_call(state, visc, rims, sector, edges):
    any_space = pl.BlockSpec(memory_space=pl.ANY)
    f32 = jnp.float32
    return pl.pallas_call(
        section_body,
        out_shape=jax.ShapeDtypeStruct((V, T, R, X), f32),
        in_specs=[any_space] * 5,
        out_specs=any_space,
        scratch_shapes=[
            pltpu.VMEM((V, T + 4, PAD, X), f32),
            pltpu.VMEM((T, R, X), f32),
            pltpu.VMEM((V, T, 4, X), f32),
            pltpu.VMEM((GROUPS, V, R, X), f32),
            pltpu.VMEM((V - 1, T, PAD, X), f32),
            pltpu.VMEM((V - 1, T + 4, R, X), f32),
            pltpu.VMEM((V, T, R, X), f32),
            pltpu.SemaphoreType.DMA((2, T // CHUNK)),
            pltpu.SemaphoreType.DMA((4,)),
            pltpu.SemaphoreType.DMA((T // CHUNK + 1,)),
        ],
        compiler_params=pltpu.CompilerParams(vmem_limit_bytes=62 * 1024 * 1024),
        cost_estimate=pl.CostEstimate(
            flops=150 * V * T * R * X // 5, bytes_accessed=24_000_000, transcendentals=T * R * X
        ),
    )(state, visc, rims, sector, edges)


def spread_table(columns):
    table = np.zeros((GROUPS * X, len(columns) * X), np.float32)
    for place, j in enumerate(columns):
        for t in range(T):
            group, slot = divmod(t, PER)
            for side in range(2):
                e = 4 + j if side == 0 else 3 - j
                table[group * X + slot * 8 + e, place * X + side * T + t] = 1
    return table


def halo_table():
    table = np.zeros((X, 4 * X), np.float32)
    for j in range(2):
        for side in range(2):
            e = 4 + j if side == 0 else 3 - j
            for slot, lane in ((1, 0), (2, T - 1)):
                table[slot * 8 + e, 2 * j * X + side * T + lane] = 1
            for slot, lane in ((0, 0), (1, 1), (2, T - 2), (3, T - 1)):
                table[slot * 8 + e, (2 * j + 1) * X + side * T + lane] = 1
    return table


def split(x):
    high = x.astype(jnp.bfloat16)
    return high, (x - high.astype(jnp.float32)).astype(jnp.bfloat16)


def dot(a, b):
    return jnp.dot(a, b, preferred_element_type=jnp.float32)


def exact_dot(x, table):
    high, low = split(x)
    return dot(high, table) + dot(low, table)


def sine(n):
    rest = n & 1023
    folded = jnp.minimum(rest, 1024 - rest).astype(jnp.float32) * (math.pi / 1024)
    s = folded * folded
    p = jnp.float32(-2.5052108e-08)
    for c in (2.7557319e-06, -1.9841270e-04, 8.3333333e-03, -1.6666667e-01, 1.0):
        p = p * s + c
    p = p * folded
    return jnp.where(n < 1024, p, -p)


def edges_body(
    n_theta, n_ax,
    state, visc, rims, spread, place, halo, coupling, block_map, plane_flags, cutoff,
    edges, sector,
    q, nu, rim, tabs, tabp, tabh, hal, packed, packed_hal, edge, around, ax_out, ax_in,
    rad, sect, send_a, recv_a, send_b, recv_b, gh, gl, lhs, filt, res,
    in_sem, misc_sem, halo_send, halo_recv, ax_send, ax_recv, a_send, a_recv, b_send, b_recv, out_sem,
):
    me = lax.axis_index("theta")
    my_ax = lax.axis_index("ax")
    nxt, prv = lax.rem(me + 1, n_theta), lax.rem(me + n_theta - 1, n_theta)
    right, left = lax.rem(my_ax + 1, n_ax), lax.rem(my_ax + n_ax - 1, n_ax)
    rs = R // n_theta

    def fetch(g):
        return pltpu.make_async_copy(
            state.at[:, pl.ds(g * PER, PER)], q.at[:, pl.ds(g * PER, PER)], in_sem.at[g]
        )

    misc = [
        pltpu.make_async_copy(rims, rim, misc_sem.at[0]),
        pltpu.make_async_copy(visc, nu, misc_sem.at[1]),
        pltpu.make_async_copy(spread, tabs, misc_sem.at[2]),
        pltpu.make_async_copy(place, tabp, misc_sem.at[3]),
        pltpu.make_async_copy(halo, tabh, misc_sem.at[4]),
    ]
    for g in range(GROUPS):
        fetch(g).start()
    for copy in misc:
        copy.start()

    barrier = pltpu.get_barrier_semaphore()

    def greet(i, carry):
        pl.semaphore_signal(
            barrier, inc=1, device_id=(lax.rem(me + i, n_theta), my_ax), device_id_type=MESH
        )
        return carry

    lax.fori_loop(1, n_theta, greet, 0)
    for other in (left, right):
        pl.semaphore_signal(barrier, inc=1, device_id=(me, other), device_id_type=MESH)
    pl.semaphore_wait(barrier, n_theta + 1)

    def to_sector(i, cells, peer):
        return pltpu.make_async_remote_copy(
            src_ref=state.at[:, cells],
            dst_ref=hal.at[i],
            send_sem=halo_send.at[i],
            recv_sem=halo_recv.at[i],
            device_id=(peer, my_ax),
            device_id_type=MESH,
        )

    halos = [to_sector(0, pl.ds(T - 2, 2), nxt), to_sector(1, pl.ds(0, 2), prv)]
    for copy in halos:
        copy.start()

    lane = lanes_of()
    slot_of = lane // 8

    def pack(load, slots):
        acc = None
        for slot in range(slots):
            turned = pltpu.roll(load(slot), (8 * slot + 4) % X, 1)
            if acc is None:
                acc = turned
            else:
                acc = jnp.where(slot_of[: turned.shape[0]] == slot, turned, acc)
        return acc

    for v in range(V + 1):
        packed[v, pl.ds(R, TILE), :] = jnp.zeros((TILE, GROUPS * X), jnp.float32)
    misc[0].wait()
    misc[1].wait()
    for g in range(GROUPS):
        cols = pl.ds(g * X, X)
        for v in range(V):
            packed[v, pl.ds(R, 4), cols] = pack(lambda t: rim[v, g * PER + t], PER)
    for g in range(GROUPS):
        fetch(g).wait()
        cols = pl.ds(g * X, X)

        def rows_of(k, carry):
            rows = pl.ds(pl.multiple_of(k * TILE, TILE), TILE)
            for v in range(V):
                packed[v, rows, cols] = pack(lambda t: q[v, g * PER + t, rows, :], PER)
            packed[V, rows, cols] = pack(lambda t: nu[g * PER + t, rows, :], PER)
            return carry

        lax.fori_loop(0, R // TILE, rows_of, 0)
    for copy in misc[2:]:
        copy.wait()

    def unpack(v, carry):
        got = exact_dot(packed[v, pl.ds(0, R + TILE), :], tabs[...])
        for j in range(4):
            edge[j, v] = got[:, j * X : (j + 1) * X]
        return carry

    lax.fori_loop(0, V + 1, unpack, 0)

    first = lane < T

    def stage(k, carry):
        rows = pl.ds(pl.multiple_of(k * TILE, TILE), TILE)
        for v in range(V):
            near, far = edge[0, v, rows, :], edge[1, v, rows, :]
            ax_out[0, v, rows, :] = jnp.where(first, near, roll(far, T))
            ax_out[1, v, rows, :] = jnp.where(first, roll(near, T), far)
        return carry

    lax.fori_loop(0, R // TILE, stage, 0)

    def to_ax(i, peer):
        return pltpu.make_async_remote_copy(
            src_ref=ax_out.at[i],
            dst_ref=ax_in.at[i],
            send_sem=ax_send.at[i],
            recv_sem=ax_recv.at[i],
            device_id=(me, peer),
            device_id_type=MESH,
        )

    sides = [to_ax(0, left), to_ax(1, right)]
    for copy in sides:
        copy.start()

    twice = 2 * cutoff[0] - 1

    def weights(b, carry):
        def some(i, carry):
            rows = pl.ds(pl.multiple_of(i * 16, 16), 16)
            down = lax.broadcasted_iota(jnp.int32, (16, 256), 0) + i * 16
            along = lax.broadcasted_iota(jnp.int32, (16, 256), 1)
            tau = (b * 256 + along - down) & 1023
            top = sine((twice * tau) & 2047)
            below = sine(jnp.maximum(tau, 1))
            ratio = jnp.where(tau == 0, twice.astype(jnp.float32), top / below)
            g = (ratio - 1.0) * (1.0 / 1024)
            high, low = split(g)
            gh[b, rows, :] = high
            gl[b, rows, :] = low
            return carry

        return lax.fori_loop(0, 16, some, carry)

    lax.fori_loop(0, 4, weights, 0)

    for copy in halos:
        copy.wait_recv()

    def pack_halo(k, carry):
        rows = pl.ds(pl.multiple_of(k * TILE, TILE), TILE)
        for v in range(V):
            packed_hal[v, rows, :] = pack(lambda t: hal[t // 2, v, t % 2, rows, :], 4)
        return carry

    lax.fori_loop(0, R // TILE, pack_halo, 0)

    def unpack_halo(v, carry):
        got = exact_dot(packed_hal[v], tabh[...])
        for i in range(4):
            around[i, v] = got[:, i * X : (i + 1) * X]
        return carry

    lax.fori_loop(0, V, unpack_halo, 0)

    to_hbm = [pltpu.make_async_copy(hal, sector, out_sem.at[0])]
    to_hbm[0].start()

    def radial(k, carry):
        rows = pl.ds(pl.multiple_of(k * TILE, TILE), TILE)
        wide = pl.ds(pl.multiple_of(k * TILE + TILE, TILE), TILE)
        for j in range(2):
            cell = [edge[j, v, rows, :] for v in range(V)]
            f = flux_r(cell, velocities(cell))
            for v in range(V):
                rad[j, v, wide, :] = f[v]
                rad[j, V + v, wide, :] = cell[v]
        return carry

    lax.fori_loop(0, R // TILE, radial, 0)
    for j in range(2):
        cell = [edge[j, v, pl.ds(R, TILE), :] for v in range(V)]
        f = flux_r(cell, velocities(cell))
        for v in range(V):
            for i, kept in ((v, f[v]), (V + v, cell[v])):
                rad[j, i, pl.ds(TILE - 2, 2), :] = kept[0:2]
                rad[j, i, pl.ds(TILE + R, 2), :] = kept[2:4]

    for copy in sides:
        copy.wait_recv()

    sign = jnp.where(first, 1.0, -1.0).astype(jnp.float32)
    has_left = (my_ax > 0).astype(jnp.int32)
    has_right = (my_ax < n_ax - 1).astype(jnp.int32)
    inside = jnp.where(first, has_left, has_right) == 1
    at = lane & (T - 1)

    def section(k, carry):
        rows = pl.ds(pl.multiple_of(k * TILE, TILE), TILE)
        low = pl.multiple_of(k * TILE, TILE)
        cells, fluxes = {}, {}
        for j in range(-2, 4):
            if j >= 0:
                cell = [edge[j, v, rows, :] for v in range(V)]
            else:
                cell = []
                for v in range(V):
                    a, b = ax_in[1, v, rows, :], ax_in[0, v, rows, :]
                    if j == -1:
                        cell.append(jnp.where(first, a, roll(b, T)))
                    else:
                        cell.append(jnp.where(first, roll(a, T), b))
            vel = velocities(cell)
            f = flux_x(cell, vel)
            if j < 0:
                f = [jnp.where(inside, x, 0.0) for x in f]
                cell = [jnp.where(inside, x, 0.0) for x in cell]
            cells[j], fluxes[j] = cell, f
        for j in range(2):
            cell = cells[j]
            f = flux_t(cell, velocities(cell))
            halo_cell = [[around[2 * j + i, v, rows, :] for v in range(V)] for i in range(2)]
            halo_flux = [flux_t(c, velocities(c)) for c in halo_cell]
            n = edge[j, V, rows, :]
            n12 = 12.0 * n
            kq = 60.0 - 72.0 * n
            for v in range(V):

                def step(o, own, near, far):
                    ends = (at >= T - o) if o > 0 else (at < -o)
                    return jnp.where(ends, near if abs(o) == 1 else far, roll(own, -o))

                def cir(o):
                    return step(o, f[v], halo_flux[0][v], halo_flux[1][v])

                def cir_cell(o):
                    return step(o, cell[v], halo_cell[0][v], halo_cell[1][v])

                def r_at(i, o):
                    return rad[j, i, pl.ds(low + TILE + o, TILE), :]

                axial = 8.0 * (fluxes[j + 1][v] - fluxes[j - 1][v]) - (
                    fluxes[j + 2][v] - fluxes[j - 2][v]
                )
                near = (r_at(v, 1) - r_at(v, -1)) + (cir(1) - cir(-1))
                far = (r_at(v, 2) - r_at(v, -2)) + (cir(2) - cir(-2))
                side = (
                    (cells[j + 1][v] + cells[j - 1][v])
                    + (r_at(V + v, 1) + r_at(V + v, -1))
                    + (cir_cell(1) + cir_cell(-1))
                )
                sect[j, v, rows, :] = UNIT * (
                    kq * cell[v] + n12 * side - sign * axial - 8.0 * near + far
                )
        return carry

    lax.fori_loop(0, R // TILE, section, 0)

    for d in range(n_theta):
        send_a[d, pl.ds(V * rs, ROWS - V * rs), :] = jnp.zeros((ROWS - V * rs, X), jnp.float32)
        for v in range(V):
            send_a[d, pl.ds(v * rs, rs), :] = sect[0, v, pl.ds(d * rs, rs), :]

    def block_copy(src, dst, sems, i):
        peer = lax.rem(me + i, n_theta)
        return pltpu.make_async_remote_copy(
            src_ref=src.at[peer],
            dst_ref=dst.at[me],
            send_sem=sems[0].at[i],
            recv_sem=sems[1].at[i],
            device_id=(peer, my_ax),
            device_id_type=MESH,
        )

    def start_all(src, dst, sems):
        def go(i, carry):
            block_copy(src, dst, sems, i).start()
            return carry

        lax.fori_loop(1, n_theta, go, 0)

    def finish_all(src, dst, sems):
        def go(i, carry):
            block_copy(src, dst, sems, i).wait()
            return carry

        lax.fori_loop(1, n_theta, go, 0)

    start_all(send_a, recv_a, (a_send, a_recv))
    recv_a[me] = send_a[me]
    finish_all(send_a, recv_a, (a_send, a_recv))

    wide_first = lanes_of(ROWS) < T
    for s in range(n_theta // 2):
        a, b = recv_a[2 * s], recv_a[2 * s + 1]
        cols = pl.ds(s * X, X)
        both = [jnp.where(wide_first, a, roll(b, T)), jnp.where(wide_first, roll(a, T), b)]
        for i in range(2):
            lhs[pl.ds(i * ROWS, ROWS), cols] = both[i]

    blocks = n_theta * T // 256
    for b in range(blocks):
        total = jnp.zeros((2 * ROWS, 256), jnp.float32)
        for a in range(blocks):
            high, low = split(lhs[:, a * 256 : (a + 1) * 256])
            k = (b - a) % blocks
            total += dot(high, gh[k]) + (dot(low, gh[k]) + dot(high, gl[k]))
        filt[:, b * 256 : (b + 1) * 256] = total

    for s in range(n_theta // 2):
        cols = pl.ds(s * X, X)
        a, b = filt[pl.ds(0, ROWS), cols], filt[pl.ds(ROWS, ROWS), cols]
        send_b[2 * s] = jnp.where(wide_first, a, roll(b, T))
        send_b[2 * s + 1] = jnp.where(wide_first, roll(a, T), b)

    start_all(send_b, recv_b, (b_send, b_recv))
    recv_b[me] = send_b[me]
    finish_all(send_b, recv_b, (b_send, b_recv))

    flag = plane_flags[block_map[my_ax]]
    on = jnp.where(lanes_of(rs) < T, lax.rem(flag, 2), lax.div(flag, 2)) == 1
    for d in range(n_theta):
        mode = [recv_b[d, pl.ds(v * rs, rs), :] for v in range(V)]
        for u in range(V):
            added = coupling[u, 0] * mode[0]
            for v in range(1, V):
                added += coupling[u, v] * mode[v]
            rows = pl.ds(d * rs, rs)
            own = sect[0, u, rows, :]
            sect[0, u, rows, :] = jnp.where(on, own + added, own)

    for v in range(V):
        both = jnp.concatenate([sect[0, v], sect[1, v]], axis=1)
        got = exact_dot(both, tabp[...])
        for g in range(GROUPS):
            res[g, v] = got[:, g * X : (g + 1) * X]
    to_hbm.append(pltpu.make_async_copy(res, edges, out_sem.at[1]))
    to_hbm[1].start()
    for copy in halos + sides:
        copy.wait_send()
    for copy in to_hbm:
        copy.wait()


def edges_call(mesh, state, visc, rims, coupling, block_map, plane_flags, cutoff):
    n_theta, n_ax = mesh.shape["theta"], mesh.shape["ax"]
    any_space = pl.BlockSpec(memory_space=pl.ANY)
    smem = pl.BlockSpec(memory_space=pltpu.SMEM)
    f32, bf16 = jnp.float32, jnp.bfloat16
    tabs = spread_table(range(4))
    tables = [jnp.asarray(x, bf16) for x in (tabs, tabs[:, : 2 * X].T, halo_table())]
    dma = pltpu.SemaphoreType.DMA
    return pl.pallas_call(
        functools.partial(edges_body, n_theta, n_ax),
        out_shape=(
            jax.ShapeDtypeStruct((GROUPS, V, R, X), f32),
            jax.ShapeDtypeStruct((2, V, 2, R, X), f32),
        ),
        in_specs=[any_space] * 6 + [smem] * 4,
        out_specs=(any_space, any_space),
        scratch_shapes=[
            pltpu.VMEM((V, T, R, X), f32),
            pltpu.VMEM((T, R, X), f32),
            pltpu.VMEM((V, T, 4, X), f32),
            pltpu.VMEM((GROUPS * X, 4 * X), bf16),
            pltpu.VMEM((2 * X, GROUPS * X), bf16),
            pltpu.VMEM((X, 4 * X), bf16),
            pltpu.VMEM((2, V, 2, R, X), f32),
            pltpu.VMEM((V + 1, R + TILE, GROUPS * X), f32),
            pltpu.VMEM((V, R, X), f32),
            pltpu.VMEM((4, V + 1, R + TILE, X), f32),
            pltpu.VMEM((4, V, R, X), f32),
            pltpu.VMEM((2, V, R, X), f32),
            pltpu.VMEM((2, V, R, X), f32),
            pltpu.VMEM((2, 2 * V, PAD, X), f32),
            pltpu.VMEM((2, V, R, X), f32),
            pltpu.VMEM((n_theta, ROWS, X), f32),
            pltpu.VMEM((n_theta, ROWS, X), f32),
            pltpu.VMEM((n_theta, ROWS, X), f32),
            pltpu.VMEM((n_theta, ROWS, X), f32),
            pltpu.VMEM((4, 256, 256), bf16),
            pltpu.VMEM((4, 256, 256), bf16),
            pltpu.VMEM((2 * ROWS, n_theta * T), f32),
            pltpu.VMEM((2 * ROWS, n_theta * T), f32),
            pltpu.VMEM((GROUPS, V, R, X), f32),
            dma((GROUPS,)),
            dma((5,)),
            dma((2,)),
            dma((2,)),
            dma((2,)),
            dma((2,)),
            dma((n_theta,)),
            dma((n_theta,)),
            dma((n_theta,)),
            dma((n_theta,)),
            dma((2,)),
        ],
        compiler_params=pltpu.CompilerParams(
            collective_id=0, has_side_effects=True, vmem_limit_bytes=56 * 1024 * 1024
        ),
        cost_estimate=pl.CostEstimate(
            flops=400_000_000, bytes_accessed=14_000_000, transcendentals=0
        ),
    )(state, visc, rims, *tables, coupling, block_map, plane_flags, cutoff)


def solution(mesh):
    def local(state, viscosity, band_rims, coupling, block_map, plane_flags, mode_cutoff):
        edges, sector = edges_call(
            mesh, state, viscosity, band_rims, coupling, block_map, plane_flags, mode_cutoff
        )
        return section_call(state, viscosity, band_rims, sector, edges)

    in_specs = (
        P(None, "theta", None, "ax"),
        P("theta", None, "ax"),
        P(None, "theta", None, "ax"),
        P(),
        P(),
        P(),
        P(),
    )
    out_specs = P(None, "theta", None, "ax")
    return jax.shard_map(local, mesh=mesh, in_specs=in_specs, out_specs=out_specs, check_vma=False)
```

```python
import functools
import math

import jax
import jax.numpy as jnp
import numpy as np
from jax import lax
from jax.experimental import pallas as pl
from jax.experimental.pallas import tpu as pltpu
from jax.sharding import PartitionSpec as P

UNIT = 0.2 / 12.0
V = 5
T = 64
R = 64
X = 128
TILE = 8
PAD = R + 2 * TILE
GROUPS = 4
PER = 16
CHUNK = 8
SHARE = 32
LAG = 3
ROWS = 24
MESH = pl.DeviceIdType.MESH


def inverse_of(density):
    guess = pl.reciprocal(density, approx=True)
    return guess * (2.0 - density * guess)


def velocities(q):
    inv = inverse_of(q[0])
    u, v, w = q[1] * inv, q[2] * inv, q[3] * inv
    p = 0.4 * (q[4] - 0.5 * (q[1] * u + q[2] * v + q[3] * w))
    return u, v, w, p, q[4] + p


def flux_x(q, vel):
    u, v, w, p, h = vel
    return [q[1], q[1] * u + p, q[2] * u, q[3] * u, h * u]


def flux_r(q, vel):
    u, v, w, p, h = vel
    return [q[2], q[2] * u, q[2] * v + p, q[3] * v, h * v]


def flux_t(q, vel):
    u, v, w, p, h = vel
    return [q[3], q[3] * u, q[3] * v, q[3] * w + p, h * w]


def roll(x, shift):
    return pltpu.roll(x, shift % X, 1)


def split(x):
    high = x.astype(jnp.bfloat16)
    return high, (x - high.astype(jnp.float32)).astype(jnp.bfloat16)


def dot(a, b):
    return jnp.dot(a, b, preferred_element_type=jnp.float32)


def stencil_table():
    table = np.zeros((X, X), np.float32)
    for x in range(X):
        for o, c in ((1, -8), (-1, 8), (2, 1), (-2, -1)):
            table[(x + o) % X, x] = c
    return np.concatenate([table, table])


def lanes_of(rows=TILE):
    return lax.broadcasted_iota(jnp.int32, (rows, X), 1)


def plane_maker(q, nu, rim, fr, ft, axial, res, stencil, turn_of=None, insert=None):
    pair = 2 * TILE

    def plane(s, first=True, second=True, circum=False, axial_before=True):
        q_near = q.at[:, pl.ds(s - LAG - 2, LAG + 3)] if second else q.at[:, pl.ds(s, 1)]
        ft_near = ft.at[:, pl.ds(s - LAG - 2, LAG + 3)] if second else ft.at[:, pl.ds(s, 1)]
        own = LAG + 2 if second else 0
        t = s - 2
        if second and first:
            fr_near, res_near, nu_near = (
                fr.at[:, pl.ds(t - LAG, LAG + 1)],
                res.at[:, pl.ds(t - LAG, LAG + 1)],
                nu.at[pl.ds(t - LAG, LAG + 1)],
            )
            new = LAG
        else:
            at = t - LAG if second else t
            if first or second:
                fr_near, res_near, nu_near = (
                    fr.at[:, pl.ds(at, 1)],
                    res.at[:, pl.ds(at, 1)],
                    nu.at[pl.ds(at, 1)],
                )
            new = 0

        def rims_of():
            for v in range(V):
                q_near[v, own, pl.ds(TILE - 2, 2), :] = rim[v, t, pl.ds(0, 2), :]
                q_near[v, own, pl.ds(TILE + R, 2), :] = rim[v, t, pl.ds(2, 2), :]
            cell = [rim[v, t, :, :] for v in range(V)]
            f = flux_r(cell, velocities(cell))
            for v in range(1, V):
                fr_near[v - 1, new, pl.ds(TILE - 2, 2), :] = f[v][0:2]
                fr_near[v - 1, new, pl.ds(TILE + R, 2), :] = f[v][2:4]

        def first_part(k):
            rows = pl.ds(k * pair, pair)
            wide = pl.ds(TILE + k * pair, pair)
            cell = [q_near[v, own, wide, :] for v in range(V)]
            vel = velocities(cell)
            f = flux_t(cell, vel)
            for v in range(1, V):
                ft_near[v - 1, own, rows, :] = f[v]
            if not first:
                return
            f = flux_x(cell, vel)
            for v in range(V):
                high, low = split(f[v])
                axial[v, rows, pl.ds(0, X)] = high
                axial[v, rows, pl.ds(X, X)] = low
            f = flux_r(cell, vel)
            for v in range(1, V):
                fr_near[v - 1, new, wide, :] = f[v]
            n = nu_near[new, rows, :]
            n12 = 12.0 * n
            kq = 60.0 - 72.0 * n
            for v in range(V):
                side = roll(cell[v], -1) + roll(cell[v], 1)
                res_near[v, new, rows, :] = kq * cell[v] + n12 * side

        if second:
            turn = turn_of(t - LAG) if insert is not None else None

        def second_part(k, v):
            rows = pl.ds(k * TILE, TILE)
            base = TILE + k * TILE
            n12 = 12.0 * nu_near[0, rows, :]

            def rad(o):
                at = pl.ds(base + o, TILE)
                return q_near[2, 2, at, :] if v == 0 else fr_near[v - 1, 0, at, :]

            def cir(o):
                if v == 0:
                    return q_near[3, 2 + o, pl.ds(base, TILE), :]
                return ft_near[v - 1, 2 + o, rows, :]

            near = (rad(1) - rad(-1)) + (cir(1) - cir(-1))
            far = (rad(2) - rad(-2)) + (cir(2) - cir(-2))
            side = (
                q_near[v, 2, pl.ds(base + 1, TILE), :] + q_near[v, 2, pl.ds(base - 1, TILE), :]
            ) + (q_near[v, 3, pl.ds(base, TILE), :] + q_near[v, 1, pl.ds(base, TILE), :])
            got = UNIT * (res_near[v, 0, rows, :] + n12 * side - 8.0 * near + far)
            if insert is not None:
                got = insert(turn, v, rows, got)
            res_near[v, 0, rows, :] = got

        if axial_before:
            before = res.at[:, pl.ds(t - 1, 1)] if new == 0 else res_near.at[:, pl.ds(new - 1, 1)]
            if second and not first:
                before = res.at[:, pl.ds(t - 1, 1)]
            for v in range(V):
                along = dot(axial[v], stencil[...])
                for k in range(R // pair):
                    rows = pl.ds(k * pair, pair)
                    before[v, 0, rows, :] += along[k * pair : (k + 1) * pair]
        if first:
            rims_of()
        for k in range(R // pair):
            if first or circum:
                first_part(k)
            if second:
                for v in range(V):
                    second_part(2 * k, v)
                    second_part(2 * k + 1, v)

    return plane


def section_body(
    state, visc, rims, sector, edges, shared, stencil, out,
    q, nu, rim, edg, fr, ft, axial, res, done, in_sem, misc_sem, out_sem, done_in, done_out,
):
    rest = T - SHARE
    n_chunks = rest // CHUNK
    portion = SHARE // n_chunks

    def fetch(c):
        t0 = c * CHUNK
        return (
            pltpu.make_async_copy(
                state.at[:, pl.ds(SHARE + t0, CHUNK)],
                q.at[:, pl.ds(t0 + 2, CHUNK), pl.ds(TILE, R)],
                in_sem.at[0, c],
            ),
            pltpu.make_async_copy(
                visc.at[pl.ds(SHARE + t0, CHUNK)], nu.at[pl.ds(t0, CHUNK)], in_sem.at[1, c]
            ),
        )

    def fetch_done(c):
        planes = pl.ds(c * portion, portion)
        return pltpu.make_async_copy(shared.at[:, planes], done.at[:, planes], done_in.at[c])

    def send_done(c):
        planes = pl.ds(c * portion, portion)
        return pltpu.make_async_copy(done.at[:, planes], out.at[:, planes], done_out.at[c])

    inner = pl.ds(TILE, R)
    misc = [
        pltpu.make_async_copy(
            state.at[:, pl.ds(SHARE - 2, 2)], q.at[:, pl.ds(0, 2), inner], misc_sem.at[0]
        ),
        pltpu.make_async_copy(sector, q.at[:, pl.ds(rest + 2, 2), inner], misc_sem.at[1]),
        pltpu.make_async_copy(rims.at[:, pl.ds(SHARE, rest)], rim, misc_sem.at[2]),
        pltpu.make_async_copy(edges, edg, misc_sem.at[3]),
    ]
    misc[0].start()
    for copy in fetch(0):
        copy.start()
    for copy in misc[1:]:
        copy.start()
    for c in range(n_chunks):
        fetch_done(c).start()
        if c + 1 < n_chunks:
            for copy in fetch(c + 1):
                copy.start()

    lane = lanes_of()
    edge_lanes = (lane < 2) | (lane >= X - 2)

    def turn_of(t):
        return t // PER, lax.rem(2 * X - 4 - 8 * lax.rem(t, PER), X)

    def insert(turn, v, rows, got):
        edge = pltpu.roll(edg[turn[0], v, rows, :], turn[1], 1)
        return jnp.where(edge_lanes, edge, got)

    plane = plane_maker(
        q, nu, rim, fr, ft, axial, res, stencil, lambda t: turn_of(t + SHARE), insert
    )

    def finish(c):
        fetch_done(c).wait()

        def one(i, carry):
            t = c * portion + i
            turn = turn_of(t)
            for v in range(V):
                for k in range(R // TILE):
                    rows = pl.ds(k * TILE, TILE)
                    done[v, t, rows, :] = insert(turn, v, rows, done[v, t, rows, :])
            return carry

        lax.fori_loop(0, portion, one, 0)
        send_done(c).start()

    def send(t0, count, c):
        return pltpu.make_async_copy(
            res.at[:, pl.ds(t0, count)], out.at[:, pl.ds(SHARE + t0, count)], out_sem.at[c]
        )

    misc[0].wait()
    plane(0, False, False, True, False)
    plane(1, False, False, True, False)
    for copy in fetch(0):
        copy.wait()
    misc[2].wait()
    misc[3].wait()
    for s in range(2, 2 + LAG):
        plane(s, True, False, axial_before=s > 2)
    plane(2 + LAG)

    def steps(low, count):
        def step(i, carry):
            plane(low + i)
            return carry

        lax.fori_loop(0, count, step, 0)

    steps(3 + LAG, CHUNK - 1 - LAG)
    send(0, CHUNK - LAG, 0).start()
    finish(0)

    def chunk(c, carry):
        for copy in fetch(c):
            copy.wait()
        steps(c * CHUNK + 2, CHUNK)
        send(c * CHUNK - LAG, CHUNK, c).start()
        finish(c)
        return carry

    lax.fori_loop(1, n_chunks, chunk, 0)
    misc[1].wait()
    plane(rest + 2, False, True, True)
    plane(rest + 3, False, True, True, False)
    plane(rest + 4, False, True, False, False)
    send(rest - LAG, LAG, n_chunks).start()
    send(0, CHUNK - LAG, 0).wait()

    def drain(c, carry):
        send(c * CHUNK - LAG, CHUNK, c).wait()
        return carry

    lax.fori_loop(1, n_chunks, drain, 0)
    send(rest - LAG, LAG, n_chunks).wait()
    for c in range(n_chunks):
        send_done(c).wait()


def section_call(state, visc, rims, sector, edges, shared, stencil):
    any_space = pl.BlockSpec(memory_space=pl.ANY)
    f32 = jnp.float32
    rest = T - SHARE
    dma = pltpu.SemaphoreType.DMA
    return pl.pallas_call(
        section_body,
        out_shape=jax.ShapeDtypeStruct((V, T, R, X), f32),
        in_specs=[any_space] * 6 + [pl.BlockSpec(memory_space=pltpu.VMEM)],
        out_specs=any_space,
        scratch_shapes=[
            pltpu.VMEM((V, rest + 5, PAD, X), f32),
            pltpu.VMEM((rest, R, X), f32),
            pltpu.VMEM((V, rest, 4, X), f32),
            pltpu.VMEM((GROUPS, V, R, X), f32),
            pltpu.VMEM((V - 1, rest, PAD, X), f32),
            pltpu.VMEM((V - 1, rest + 5, R, X), f32),
            pltpu.VMEM((V, R, 2 * X), jnp.bfloat16),
            pltpu.VMEM((V, rest, R, X), f32),
            pltpu.VMEM((V, SHARE, R, X), f32),
            dma((2, rest // CHUNK)),
            dma((4,)),
            dma((rest // CHUNK + 1,)),
            dma((rest // CHUNK,)),
            dma((rest // CHUNK,)),
        ],
        compiler_params=pltpu.CompilerParams(vmem_limit_bytes=60 * 1024 * 1024),
        cost_estimate=pl.CostEstimate(
            flops=150 * rest * R * X, bytes_accessed=24_000_000, transcendentals=rest * R * X
        ),
    )(state, visc, rims, sector, edges, shared, stencil)


def spread_table(columns):
    table = np.zeros((GROUPS * X, len(columns) * X), np.float32)
    for place, j in enumerate(columns):
        for t in range(T):
            group, slot = divmod(t, PER)
            for side in range(2):
                e = 4 + j if side == 0 else 3 - j
                table[group * X + slot * 8 + e, place * X + side * T + t] = 1
    return table


def halo_table():
    table = np.zeros((X, 4 * X), np.float32)
    for j in range(2):
        for side in range(2):
            e = 4 + j if side == 0 else 3 - j
            for slot, lane in ((1, 0), (2, T - 1)):
                table[slot * 8 + e, 2 * j * X + side * T + lane] = 1
            for slot, lane in ((0, 0), (1, 1), (2, T - 2), (3, T - 1)):
                table[slot * 8 + e, (2 * j + 1) * X + side * T + lane] = 1
    return table


def exact_dot(x, table):
    high, low = split(x)
    return dot(high, table) + dot(low, table)


def sine(n):
    rest = n & 1023
    folded = jnp.minimum(rest, 1024 - rest).astype(jnp.float32) * (math.pi / 1024)
    s = folded * folded
    p = jnp.float32(-2.5052108e-08)
    for c in (2.7557319e-06, -1.9841270e-04, 8.3333333e-03, -1.6666667e-01, 1.0):
        p = p * s + c
    p = p * folded
    return jnp.where(n < 1024, p, -p)


PARTS = (2 + LAG, 12, 24, SHARE + LAG + 2)


def edges_body(
    n_theta, n_ax,
    state, visc, rims, spread, place, halo, stencil, coupling, block_map, plane_flags, cutoff,
    edges, sector, shared,
    q, nu, rim, fr, ft, axial, out, tabs, tabp, tabh, packed, packed_hal, edge, around, ax_out, ax_in,
    rad, sect, send_a, recv_a, send_b, recv_b, gh, gl, lhs, filt, res,
    in_sem, misc_sem, halo_send, halo_recv, ax_send, ax_recv, a_send, a_recv, b_send, b_recv, out_sem,
):
    me = lax.axis_index("theta")
    my_ax = lax.axis_index("ax")
    nxt, prv = lax.rem(me + 1, n_theta), lax.rem(me + n_theta - 1, n_theta)
    right, left = lax.rem(my_ax + 1, n_ax), lax.rem(my_ax + n_ax - 1, n_ax)
    rs = R // n_theta

    def fetch(g):
        return pltpu.make_async_copy(
            state.at[:, pl.ds(g * PER, PER)],
            q.at[:, pl.ds(2 + g * PER, PER), pl.ds(TILE, R)],
            in_sem.at[g],
        )

    misc = [
        pltpu.make_async_copy(rims, rim, misc_sem.at[0]),
        pltpu.make_async_copy(visc, nu, misc_sem.at[1]),
        pltpu.make_async_copy(spread, tabs, misc_sem.at[2]),
        pltpu.make_async_copy(place, tabp, misc_sem.at[3]),
        pltpu.make_async_copy(halo, tabh, misc_sem.at[4]),
    ]
    for g in range(GROUPS):
        fetch(g).start()
    for copy in misc:
        copy.start()

    barrier = pltpu.get_barrier_semaphore()

    def greet(i, carry):
        pl.semaphore_signal(
            barrier, inc=1, device_id=(lax.rem(me + i, n_theta), my_ax), device_id_type=MESH
        )
        return carry

    lax.fori_loop(1, n_theta, greet, 0)
    for other in (left, right):
        pl.semaphore_signal(barrier, inc=1, device_id=(me, other), device_id_type=MESH)
    twice = 2 * cutoff[0] - 1

    def weights(b, carry):
        def some(i, carry):
            rows = pl.ds(pl.multiple_of(i * 16, 16), 16)
            down = lax.broadcasted_iota(jnp.int32, (16, 256), 0) + i * 16
            along = lax.broadcasted_iota(jnp.int32, (16, 256), 1)
            tau = (b * 256 + along - down) & 1023
            top = sine((twice * tau) & 2047)
            below = sine(jnp.maximum(tau, 1))
            ratio = jnp.where(tau == 0, twice.astype(jnp.float32), top / below)
            g = (ratio - 1.0) * (1.0 / 1024)
            high, low = split(g)
            gh[b, rows, :] = high
            gl[b, rows, :] = low
            return carry

        return lax.fori_loop(0, 16, some, carry)

    lax.fori_loop(0, 4, weights, 0)

    pl.semaphore_wait(barrier, n_theta + 1)

    def to_sector(i, cells, peer):
        return pltpu.make_async_remote_copy(
            src_ref=state.at[:, cells],
            dst_ref=q.at[:, pl.ds(i * (T + 2), 2), pl.ds(TILE, R)],
            send_sem=halo_send.at[i],
            recv_sem=halo_recv.at[i],
            device_id=(peer, my_ax),
            device_id_type=MESH,
        )

    halos = [to_sector(0, pl.ds(T - 2, 2), nxt), to_sector(1, pl.ds(0, 2), prv)]
    for copy in halos:
        copy.start()

    lane = lanes_of()
    slot_of = lane // 8

    def pack(load, slots):
        acc = None
        for slot in range(slots):
            turned = pltpu.roll(load(slot), (8 * slot + 4) % X, 1)
            if acc is None:
                acc = turned
            else:
                acc = jnp.where(slot_of[: turned.shape[0]] == slot, turned, acc)
        return acc

    for v in range(V + 1):
        packed[v, pl.ds(R, TILE), :] = jnp.zeros((TILE, GROUPS * X), jnp.float32)
    misc[0].wait()
    misc[1].wait()
    for g in range(GROUPS):
        cols = pl.ds(g * X, X)
        for v in range(V):
            packed[v, pl.ds(R, 4), cols] = pack(lambda t: rim[v, g * PER + t], PER)
    for g in range(GROUPS):
        fetch(g).wait()
        cols = pl.ds(g * X, X)

        def rows_of(k, carry):
            rows = pl.ds(pl.multiple_of(k * TILE, TILE), TILE)
            wide = pl.ds(pl.multiple_of(k * TILE + TILE, TILE), TILE)
            for v in range(V):
                packed[v, rows, cols] = pack(lambda t: q[v, 2 + g * PER + t, wide, :], PER)
            packed[V, rows, cols] = pack(lambda t: nu[g * PER + t, rows, :], PER)
            return carry

        lax.fori_loop(0, R // TILE, rows_of, 0)
    for copy in misc[2:]:
        copy.wait()

    def unpack(v, carry):
        got = exact_dot(packed[v, pl.ds(0, R + TILE), :], tabs[...])
        for j in range(4):
            edge[j, v] = got[:, j * X : (j + 1) * X]
        return carry

    lax.fori_loop(0, V + 1, unpack, 0)

    first = lane < T

    def stage(k, carry):
        rows = pl.ds(pl.multiple_of(k * TILE, TILE), TILE)
        for v in range(V):
            near, far = edge[0, v, rows, :], edge[1, v, rows, :]
            ax_out[0, v, rows, :] = jnp.where(first, near, roll(far, T))
            ax_out[1, v, rows, :] = jnp.where(first, roll(near, T), far)
        return carry

    lax.fori_loop(0, R // TILE, stage, 0)

    def to_ax(i, peer):
        return pltpu.make_async_remote_copy(
            src_ref=ax_out.at[i],
            dst_ref=ax_in.at[i],
            send_sem=ax_send.at[i],
            recv_sem=ax_recv.at[i],
            device_id=(me, peer),
            device_id_type=MESH,
        )

    sides = [to_ax(0, left), to_ax(1, right)]
    for copy in sides:
        copy.start()

    for copy in halos:
        copy.wait_recv()

    def pack_halo(k, carry):
        rows = pl.ds(pl.multiple_of(k * TILE, TILE), TILE)
        wide = pl.ds(pl.multiple_of(k * TILE + TILE, TILE), TILE)
        for v in range(V):
            packed_hal[v, rows, :] = pack(lambda t: q[v, t + T * (t // 2), wide, :], 4)
        return carry

    lax.fori_loop(0, R // TILE, pack_halo, 0)

    def unpack_halo(v, carry):
        got = exact_dot(packed_hal[v], tabh[...])
        for i in range(4):
            around[i, v] = got[:, i * X : (i + 1) * X]
        return carry

    lax.fori_loop(0, V, unpack_halo, 0)

    to_hbm = [
        pltpu.make_async_copy(
            q.at[:, pl.ds(T + 2, 2), pl.ds(TILE, R)], sector, out_sem.at[0]
        )
    ]
    to_hbm[0].start()

    def radial(k, carry):
        rows = pl.ds(pl.multiple_of(k * TILE, TILE), TILE)
        wide = pl.ds(pl.multiple_of(k * TILE + TILE, TILE), TILE)
        for j in range(2):
            cell = [edge[j, v, rows, :] for v in range(V)]
            f = flux_r(cell, velocities(cell))
            for v in range(V):
                rad[j, v, wide, :] = f[v]
                rad[j, V + v, wide, :] = cell[v]
        return carry

    lax.fori_loop(0, R // TILE, radial, 0)
    for j in range(2):
        cell = [edge[j, v, pl.ds(R, TILE), :] for v in range(V)]
        f = flux_r(cell, velocities(cell))
        for v in range(V):
            for i, kept in ((v, f[v]), (V + v, cell[v])):
                rad[j, i, pl.ds(TILE - 2, 2), :] = kept[0:2]
                rad[j, i, pl.ds(TILE + R, 2), :] = kept[2:4]

    plane = plane_maker(q, nu, rim, fr, ft, axial, out, stencil)

    def planes(part):
        low, high = PARTS[part], PARTS[part + 1]

        def step(s, carry):
            plane(s)
            return carry

        lax.fori_loop(low, high, step, 0)
        t0, t1 = (0 if part == 0 else low - 2 - LAG), high - 2 - LAG
        copy = pltpu.make_async_copy(
            out.at[:, pl.ds(t0, t1 - t0)], shared.at[:, pl.ds(t0, t1 - t0)], out_sem.at[2 + part]
        )
        copy.start()
        to_hbm.append(copy)

    plane(0, False, False, True, False)
    plane(1, False, False, True, False)
    for s in range(2, 2 + LAG):
        plane(s, True, False, axial_before=s > 2)
    planes(0)

    for copy in sides:
        copy.wait_recv()

    sign = jnp.where(first, 1.0, -1.0).astype(jnp.float32)
    has_left = (my_ax > 0).astype(jnp.int32)
    has_right = (my_ax < n_ax - 1).astype(jnp.int32)
    inside = jnp.where(first, has_left, has_right) == 1
    at = lane & (T - 1)

    def section(k, carry):
        rows = pl.ds(pl.multiple_of(k * TILE, TILE), TILE)
        low = pl.multiple_of(k * TILE, TILE)
        cells, fluxes = {}, {}
        for j in range(-2, 4):
            if j >= 0:
                cell = [edge[j, v, rows, :] for v in range(V)]
            else:
                cell = []
                for v in range(V):
                    a, b = ax_in[1, v, rows, :], ax_in[0, v, rows, :]
                    if j == -1:
                        cell.append(jnp.where(first, a, roll(b, T)))
                    else:
                        cell.append(jnp.where(first, roll(a, T), b))
            vel = velocities(cell)
            f = flux_x(cell, vel)
            if j < 0:
                f = [jnp.where(inside, x, 0.0) for x in f]
                cell = [jnp.where(inside, x, 0.0) for x in cell]
            cells[j], fluxes[j] = cell, f
        for j in range(2):
            cell = cells[j]
            f = flux_t(cell, velocities(cell))
            halo_cell = [[around[2 * j + i, v, rows, :] for v in range(V)] for i in range(2)]
            halo_flux = [flux_t(c, velocities(c)) for c in halo_cell]
            n = edge[j, V, rows, :]
            n12 = 12.0 * n
            kq = 60.0 - 72.0 * n
            for v in range(V):

                def step(o, own, near, far):
                    ends = (at >= T - o) if o > 0 else (at < -o)
                    return jnp.where(ends, near if abs(o) == 1 else far, roll(own, -o))

                def cir(o):
                    return step(o, f[v], halo_flux[0][v], halo_flux[1][v])

                def cir_cell(o):
                    return step(o, cell[v], halo_cell[0][v], halo_cell[1][v])

                def r_at(i, o):
                    return rad[j, i, pl.ds(low + TILE + o, TILE), :]

                axial = 8.0 * (fluxes[j + 1][v] - fluxes[j - 1][v]) - (
                    fluxes[j + 2][v] - fluxes[j - 2][v]
                )
                near = (r_at(v, 1) - r_at(v, -1)) + (cir(1) - cir(-1))
                far = (r_at(v, 2) - r_at(v, -2)) + (cir(2) - cir(-2))
                side = (
                    (cells[j + 1][v] + cells[j - 1][v])
                    + (r_at(V + v, 1) + r_at(V + v, -1))
                    + (cir_cell(1) + cir_cell(-1))
                )
                sect[j, v, rows, :] = UNIT * (
                    kq * cell[v] + n12 * side - sign * axial - 8.0 * near + far
                )
        return carry

    lax.fori_loop(0, R // TILE, section, 0)

    for d in range(n_theta):
        send_a[d, pl.ds(V * rs, ROWS - V * rs), :] = jnp.zeros((ROWS - V * rs, X), jnp.float32)
        for v in range(V):
            send_a[d, pl.ds(v * rs, rs), :] = sect[0, v, pl.ds(d * rs, rs), :]

    def block_copy(src, dst, sems, i):
        peer = lax.rem(me + i, n_theta)
        return pltpu.make_async_remote_copy(
            src_ref=src.at[peer],
            dst_ref=dst.at[me],
            send_sem=sems[0].at[i],
            recv_sem=sems[1].at[i],
            device_id=(peer, my_ax),
            device_id_type=MESH,
        )

    def start_all(src, dst, sems):
        def go(i, carry):
            block_copy(src, dst, sems, i).start()
            return carry

        lax.fori_loop(1, n_theta, go, 0)

    def finish_all(src, dst, sems):
        def go(i, carry):
            block_copy(src, dst, sems, i).wait()
            return carry

        lax.fori_loop(1, n_theta, go, 0)

    start_all(send_a, recv_a, (a_send, a_recv))
    recv_a[me] = send_a[me]
    planes(1)
    finish_all(send_a, recv_a, (a_send, a_recv))

    wide_first = lanes_of(ROWS) < T
    for s in range(n_theta // 2):
        a, b = recv_a[2 * s], recv_a[2 * s + 1]
        cols = pl.ds(s * X, X)
        both = [jnp.where(wide_first, a, roll(b, T)), jnp.where(wide_first, roll(a, T), b)]
        for i in range(2):
            high, low = split(both[i])
            lhs[pl.ds(i * ROWS, ROWS), cols] = high.astype(jnp.float32)
            lhs[pl.ds((2 + i) * ROWS, ROWS), cols] = low.astype(jnp.float32)

    blocks = n_theta * T // 256
    terms = [lhs[:, a * 256 : (a + 1) * 256].astype(jnp.bfloat16) for a in range(blocks)]
    for b in range(blocks):
        total = None
        for a in range(blocks):
            k = (b - a) % blocks
            wide = dot(terms[a], gh[k])
            term = (wide[: 2 * ROWS] + wide[2 * ROWS :]) + dot(terms[a][: 2 * ROWS], gl[k])
            total = term if total is None else total + term
        filt[:, b * 256 : (b + 1) * 256] = total

    for s in range(n_theta // 2):
        cols = pl.ds(s * X, X)
        a, b = filt[pl.ds(0, ROWS), cols], filt[pl.ds(ROWS, ROWS), cols]
        send_b[2 * s] = jnp.where(wide_first, a, roll(b, T))
        send_b[2 * s + 1] = jnp.where(wide_first, roll(a, T), b)

    start_all(send_b, recv_b, (b_send, b_recv))
    recv_b[me] = send_b[me]
    planes(2)
    finish_all(send_b, recv_b, (b_send, b_recv))

    flag = plane_flags[block_map[my_ax]]
    on = jnp.where(lanes_of(rs) < T, lax.rem(flag, 2), lax.div(flag, 2)) == 1
    for d in range(n_theta):
        mode = [recv_b[d, pl.ds(v * rs, rs), :] for v in range(V)]
        for u in range(V):
            added = coupling[u, 0] * mode[0]
            for v in range(1, V):
                added += coupling[u, v] * mode[v]
            rows = pl.ds(d * rs, rs)
            own = sect[0, u, rows, :]
            sect[0, u, rows, :] = jnp.where(on, own + added, own)

    for v in range(V):
        both = jnp.concatenate([sect[0, v], sect[1, v]], axis=1)
        got = exact_dot(both, tabp[...])
        for g in range(GROUPS):
            res[g, v] = got[:, g * X : (g + 1) * X]
    to_hbm.append(pltpu.make_async_copy(res, edges, out_sem.at[1]))
    to_hbm[-1].start()
    for copy in halos + sides:
        copy.wait_send()
    for copy in to_hbm:
        copy.wait()


def edges_call(mesh, state, visc, rims, stencil, coupling, block_map, plane_flags, cutoff):
    n_theta, n_ax = mesh.shape["theta"], mesh.shape["ax"]
    any_space = pl.BlockSpec(memory_space=pl.ANY)
    smem = pl.BlockSpec(memory_space=pltpu.SMEM)
    f32, bf16 = jnp.float32, jnp.bfloat16
    tabs = spread_table(range(4))
    tables = [jnp.asarray(x, bf16) for x in (tabs, tabs[:, : 2 * X].T, halo_table())]
    dma = pltpu.SemaphoreType.DMA
    return pl.pallas_call(
        functools.partial(edges_body, n_theta, n_ax),
        out_shape=(
            jax.ShapeDtypeStruct((GROUPS, V, R, X), f32),
            jax.ShapeDtypeStruct((V, 2, R, X), f32),
            jax.ShapeDtypeStruct((V, SHARE, R, X), f32),
        ),
        in_specs=[any_space] * 6 + [pl.BlockSpec(memory_space=pltpu.VMEM)] + [smem] * 4,
        out_specs=(any_space, any_space, any_space),
        scratch_shapes=[
            pltpu.VMEM((V, T + 4, PAD, X), f32),
            pltpu.VMEM((T, R, X), f32),
            pltpu.VMEM((V, T, 4, X), f32),
            pltpu.VMEM((V - 1, SHARE + LAG, PAD, X), f32),
            pltpu.VMEM((V - 1, SHARE + LAG + 2, R, X), f32),
            pltpu.VMEM((V, R, 2 * X), bf16),
            pltpu.VMEM((V, SHARE + LAG, R, X), f32),
            pltpu.VMEM((GROUPS * X, 4 * X), bf16),
            pltpu.VMEM((2 * X, GROUPS * X), bf16),
            pltpu.VMEM((X, 4 * X), bf16),
            pltpu.VMEM((V + 1, R + TILE, GROUPS * X), f32),
            pltpu.VMEM((V, R, X), f32),
            pltpu.VMEM((4, V + 1, R + TILE, X), f32),
            pltpu.VMEM((4, V, R, X), f32),
            pltpu.VMEM((2, V, R, X), f32),
            pltpu.VMEM((2, V, R, X), f32),
            pltpu.VMEM((2, 2 * V, PAD, X), f32),
            pltpu.VMEM((2, V, R, X), f32),
            pltpu.VMEM((n_theta, ROWS, X), f32),
            pltpu.VMEM((n_theta, ROWS, X), f32),
            pltpu.VMEM((n_theta, ROWS, X), f32),
            pltpu.VMEM((n_theta, ROWS, X), f32),
            pltpu.VMEM((4, 256, 256), bf16),
            pltpu.VMEM((4, 256, 256), bf16),
            pltpu.VMEM((4 * ROWS, n_theta * T), f32),
            pltpu.VMEM((2 * ROWS, n_theta * T), f32),
            pltpu.VMEM((GROUPS, V, R, X), f32),
            dma((GROUPS,)),
            dma((5,)),
            dma((2,)),
            dma((2,)),
            dma((2,)),
            dma((2,)),
            dma((n_theta,)),
            dma((n_theta,)),
            dma((n_theta,)),
            dma((n_theta,)),
            dma((5,)),
        ],
        compiler_params=pltpu.CompilerParams(
            collective_id=0, has_side_effects=True, vmem_limit_bytes=60 * 1024 * 1024
        ),
        cost_estimate=pl.CostEstimate(
            flops=400_000_000, bytes_accessed=14_000_000, transcendentals=0
        ),
    )(state, visc, rims, *tables, stencil, coupling, block_map, plane_flags, cutoff)


def solution(mesh):
    def local(state, viscosity, band_rims, coupling, block_map, plane_flags, mode_cutoff):
        stencil = jnp.asarray(stencil_table(), jnp.bfloat16)
        edges, sector, shared = edges_call(
            mesh,
            state,
            viscosity,
            band_rims,
            stencil,
            coupling,
            block_map,
            plane_flags,
            mode_cutoff,
        )
        return section_call(state, viscosity, band_rims, sector, edges, shared, stencil)

    in_specs = (
        P(None, "theta", None, "ax"),
        P("theta", None, "ax"),
        P(None, "theta", None, "ax"),
        P(),
        P(),
        P(),
        P(),
    )
    out_specs = P(None, "theta", None, "ax")
    return jax.shard_map(local, mesh=mesh, in_specs=in_specs, out_specs=out_specs, check_vma=False)
```

```python
import functools
import math

import jax
import jax.numpy as jnp
import numpy as np
from jax import lax
from jax.experimental import pallas as pl
from jax.experimental.pallas import tpu as pltpu
from jax.sharding import PartitionSpec as P

UNIT = 0.2 / 12.0
V = 5
T = 64
R = 64
X = 128
TILE = 8
PAD = R + 2 * TILE
GROUPS = 4
PER = 16
CHUNK = 8
SHARE = 40
LAG = 3
ROWS = 24
MESH = pl.DeviceIdType.MESH


def inverse_of(density):
    guess = pl.reciprocal(density, approx=True)
    return guess * (2.0 - density * guess)


def velocities(q):
    inv = inverse_of(q[0])
    u, v, w = q[1] * inv, q[2] * inv, q[3] * inv
    p = 0.4 * (q[4] - 0.5 * (q[1] * u + q[2] * v + q[3] * w))
    return u, v, w, p, q[4] + p


def flux_x(q, vel):
    u, v, w, p, h = vel
    return [q[1], q[1] * u + p, q[2] * u, q[3] * u, h * u]


def flux_r(q, vel):
    u, v, w, p, h = vel
    return [q[2], q[2] * u, q[2] * v + p, q[3] * v, h * v]


def flux_t(q, vel):
    u, v, w, p, h = vel
    return [q[3], q[3] * u, q[3] * v, q[3] * w + p, h * w]


def roll(x, shift):
    return pltpu.roll(x, shift % X, 1)


def split(x):
    high = x.astype(jnp.bfloat16)
    return high, (x - high.astype(jnp.float32)).astype(jnp.bfloat16)


def dot(a, b):
    return jnp.dot(a, b, preferred_element_type=jnp.float32)


def stencil_table():
    table = np.zeros((X, X), np.float32)
    for x in range(X):
        for o, c in ((1, -8), (-1, 8), (2, 1), (-2, -1)):
            table[(x + o) % X, x] = c
    return np.concatenate([table, table])


def lanes_of(rows=TILE):
    return lax.broadcasted_iota(jnp.int32, (rows, X), 1)


def plane_maker(q, nu, rim, fr, ft, axial, res, stencil, turn_of=None, insert=None):
    pair = 2 * TILE

    def plane(s, first=True, second=True, circum=False, axial_before=True):
        q_near = q.at[:, pl.ds(s - LAG - 2, LAG + 3)] if second else q.at[:, pl.ds(s, 1)]
        ft_near = ft.at[:, pl.ds(s - LAG - 2, LAG + 3)] if second else ft.at[:, pl.ds(s, 1)]
        own = LAG + 2 if second else 0
        t = s - 2
        if second and first:
            fr_near, res_near, nu_near = (
                fr.at[:, pl.ds(t - LAG, LAG + 1)],
                res.at[:, pl.ds(t - LAG, LAG + 1)],
                nu.at[pl.ds(t - LAG, LAG + 1)],
            )
            new = LAG
        else:
            at = t - LAG if second else t
            if first or second:
                fr_near, res_near, nu_near = (
                    fr.at[:, pl.ds(at, 1)],
                    res.at[:, pl.ds(at, 1)],
                    nu.at[pl.ds(at, 1)],
                )
            new = 0

        def rims_of():
            for v in range(V):
                q_near[v, own, pl.ds(TILE - 2, 2), :] = rim[v, t, pl.ds(0, 2), :]
                q_near[v, own, pl.ds(TILE + R, 2), :] = rim[v, t, pl.ds(2, 2), :]
            cell = [rim[v, t, :, :] for v in range(V)]
            f = flux_r(cell, velocities(cell))
            for v in range(1, V):
                fr_near[v - 1, new, pl.ds(TILE - 2, 2), :] = f[v][0:2]
                fr_near[v - 1, new, pl.ds(TILE + R, 2), :] = f[v][2:4]

        def first_part(k):
            rows = pl.ds(k * pair, pair)
            wide = pl.ds(TILE + k * pair, pair)
            cell = [q_near[v, own, wide, :] for v in range(V)]
            vel = velocities(cell)
            f = flux_t(cell, vel)
            for v in range(1, V):
                ft_near[v - 1, own, rows, :] = f[v]
            if not first:
                return
            f = flux_x(cell, vel)
            for v in range(V):
                high, low = split(f[v])
                axial[v, rows, pl.ds(0, X)] = high
                axial[v, rows, pl.ds(X, X)] = low
            f = flux_r(cell, vel)
            for v in range(1, V):
                fr_near[v - 1, new, wide, :] = f[v]
            n = nu_near[new, rows, :]
            n12 = 12.0 * n
            kq = 60.0 - 72.0 * n
            for v in range(V):
                side = roll(cell[v], -1) + roll(cell[v], 1)
                res_near[v, new, rows, :] = kq * cell[v] + n12 * side

        if second:
            turn = turn_of(t - LAG) if insert is not None else None

        def second_part(k, v):
            rows = pl.ds(k * TILE, TILE)
            base = TILE + k * TILE
            n12 = 12.0 * nu_near[0, rows, :]

            def rad(o):
                at = pl.ds(base + o, TILE)
                return q_near[2, 2, at, :] if v == 0 else fr_near[v - 1, 0, at, :]

            def cir(o):
                if v == 0:
                    return q_near[3, 2 + o, pl.ds(base, TILE), :]
                return ft_near[v - 1, 2 + o, rows, :]

            near = (rad(1) - rad(-1)) + (cir(1) - cir(-1))
            far = (rad(2) - rad(-2)) + (cir(2) - cir(-2))
            side = (
                q_near[v, 2, pl.ds(base + 1, TILE), :] + q_near[v, 2, pl.ds(base - 1, TILE), :]
            ) + (q_near[v, 3, pl.ds(base, TILE), :] + q_near[v, 1, pl.ds(base, TILE), :])
            got = UNIT * (res_near[v, 0, rows, :] + n12 * side - 8.0 * near + far)
            if insert is not None:
                got = insert(turn, v, rows, got)
            res_near[v, 0, rows, :] = got

        if axial_before:
            before = res.at[:, pl.ds(t - 1, 1)] if new == 0 else res_near.at[:, pl.ds(new - 1, 1)]
            if second and not first:
                before = res.at[:, pl.ds(t - 1, 1)]
            for v in range(V):
                along = dot(axial[v], stencil[...])
                for k in range(R // pair):
                    rows = pl.ds(k * pair, pair)
                    before[v, 0, rows, :] += along[k * pair : (k + 1) * pair]
        if first:
            rims_of()
        for k in range(R // pair):
            if first or circum:
                first_part(k)
            if second:
                for v in range(V):
                    second_part(2 * k, v)
                    second_part(2 * k + 1, v)

    return plane


def section_body(
    state, visc, rims, sector, edges, shared, stencil, out,
    q, nu, rim, edg, fr, ft, axial, res, done, in_sem, misc_sem, out_sem, done_in, done_out,
):
    rest = T - SHARE
    n_chunks = rest // CHUNK

    def fetch(c):
        t0 = c * CHUNK
        return (
            pltpu.make_async_copy(
                state.at[:, pl.ds(SHARE + t0, CHUNK)],
                q.at[:, pl.ds(t0 + 2, CHUNK), pl.ds(TILE, R)],
                in_sem.at[0, c],
            ),
            pltpu.make_async_copy(
                visc.at[pl.ds(SHARE + t0, CHUNK)], nu.at[pl.ds(t0, CHUNK)], in_sem.at[1, c]
            ),
        )

    head = CHUNK - 1 - LAG
    each = SHARE // (rest - CHUNK + head)
    portions = [(0, head * each)]
    portions += [((head + CHUNK * (c - 1)) * each, CHUNK * each) for c in range(1, n_chunks)]

    def fetch_part(t0, count, c):
        planes = pl.ds(t0, count)
        return pltpu.make_async_copy(shared.at[:, planes], done.at[:, planes], done_in.at[c])

    def send_part(t0, count, c):
        planes = pl.ds(t0, count)
        return pltpu.make_async_copy(done.at[:, planes], out.at[:, planes], done_out.at[c])

    inner = pl.ds(TILE, R)
    misc = [
        pltpu.make_async_copy(
            state.at[:, pl.ds(SHARE - 2, 2)], q.at[:, pl.ds(0, 2), inner], misc_sem.at[0]
        ),
        pltpu.make_async_copy(sector, q.at[:, pl.ds(rest + 2, 2), inner], misc_sem.at[1]),
        pltpu.make_async_copy(rims.at[:, pl.ds(SHARE, rest)], rim, misc_sem.at[2]),
        pltpu.make_async_copy(edges, edg, misc_sem.at[3]),
    ]
    misc[0].start()
    misc[2].start()
    for copy in fetch(0):
        copy.start()
    misc[3].start()
    fetch_part(*portions[0], 0).start()
    for c in range(1, n_chunks):
        for copy in fetch(c):
            copy.start()
        fetch_part(*portions[c], c).start()
    misc[1].start()

    lane = lanes_of()
    edge_lanes = (lane < 2) | (lane >= X - 2)

    def turn_of(t):
        return t // PER, lax.rem(2 * X - 4 - 8 * lax.rem(t, PER), X)

    def insert(turn, v, rows, got):
        edge = pltpu.roll(edg[turn[0], v, rows, :], turn[1], 1)
        return jnp.where(edge_lanes, edge, got)

    plane = plane_maker(
        q, nu, rim, fr, ft, axial, res, stencil, lambda t: turn_of(t + SHARE), insert
    )

    def finish(t):
        turn = turn_of(t)
        near = done.at[:, pl.ds(t, 1)]
        for v in range(V):
            for k in range(R // TILE):
                rows = pl.ds(k * TILE, TILE)
                near[v, 0, rows, :] = insert(turn, v, rows, near[v, 0, rows, :])

    def send(t0, count, c):
        return pltpu.make_async_copy(
            res.at[:, pl.ds(t0, count)], out.at[:, pl.ds(SHARE + t0, count)], out_sem.at[c]
        )

    misc[0].wait()
    plane(0, False, False, True, False)
    plane(1, False, False, True, False)
    misc[2].wait()
    for copy in fetch(0):
        copy.wait()
    for s in range(2, 2 + LAG):
        plane(s, True, False, axial_before=s > 2)
    misc[3].wait()
    plane(2 + LAG)

    def steps(low, count):
        def step(i, carry):
            plane(low + i)
            for j in range(each):
                finish((low + i - 3 - LAG) * each + j)
            return carry

        lax.fori_loop(0, count, step, 0)

    fetch_part(*portions[0], 0).wait()
    steps(3 + LAG, head)
    send(0, CHUNK - LAG, 0).start()
    send_part(*portions[0], 0).start()

    def chunk(c, carry):
        for copy in fetch(c):
            copy.wait()
        t0 = (head + CHUNK * (c - 1)) * each
        fetch_part(t0, CHUNK * each, c).wait()
        steps(c * CHUNK + 2, CHUNK)
        send(c * CHUNK - LAG, CHUNK, c).start()
        send_part(t0, CHUNK * each, c).start()
        return carry

    lax.fori_loop(1, n_chunks, chunk, 0)
    misc[1].wait()
    for i in range(LAG):
        plane(rest + 2 + i, False, True, i < 2, i < 1)
    send(rest - LAG, LAG, n_chunks).start()
    send(0, CHUNK - LAG, 0).wait()

    def drain(c, carry):
        send(c * CHUNK - LAG, CHUNK, c).wait()
        send_part((head + CHUNK * (c - 1)) * each, CHUNK * each, c).wait()
        return carry

    lax.fori_loop(1, n_chunks, drain, 0)
    send_part(*portions[0], 0).wait()
    send(rest - LAG, LAG, n_chunks).wait()


def section_call(state, visc, rims, sector, edges, shared, stencil):
    any_space = pl.BlockSpec(memory_space=pl.ANY)
    f32 = jnp.float32
    rest = T - SHARE
    dma = pltpu.SemaphoreType.DMA
    return pl.pallas_call(
        section_body,
        out_shape=jax.ShapeDtypeStruct((V, T, R, X), f32),
        in_specs=[any_space] * 6 + [pl.BlockSpec(memory_space=pltpu.VMEM)],
        out_specs=any_space,
        scratch_shapes=[
            pltpu.VMEM((V, rest + 5, PAD, X), f32),
            pltpu.VMEM((rest, R, X), f32),
            pltpu.VMEM((V, rest, 4, X), f32),
            pltpu.VMEM((GROUPS, V, R, X), f32),
            pltpu.VMEM((V - 1, rest, PAD, X), f32),
            pltpu.VMEM((V - 1, rest + 5, R, X), f32),
            pltpu.VMEM((V, R, 2 * X), jnp.bfloat16),
            pltpu.VMEM((V, rest, R, X), f32),
            pltpu.VMEM((V, SHARE, R, X), f32),
            dma((2, rest // CHUNK)),
            dma((4,)),
            dma((rest // CHUNK + 1,)),
            dma((rest // CHUNK,)),
            dma((rest // CHUNK,)),
        ],
        compiler_params=pltpu.CompilerParams(vmem_limit_bytes=60 * 1024 * 1024),
        cost_estimate=pl.CostEstimate(
            flops=150 * rest * R * X, bytes_accessed=24_000_000, transcendentals=rest * R * X
        ),
    )(state, visc, rims, sector, edges, shared, stencil)


def spread_table(columns):
    table = np.zeros((GROUPS * X, len(columns) * X), np.float32)
    for place, j in enumerate(columns):
        for t in range(T):
            group, slot = divmod(t, PER)
            for side in range(2):
                e = 4 + j if side == 0 else 3 - j
                table[group * X + slot * 8 + e, place * X + side * T + t] = 1
    return table


def pick_table():
    table = np.zeros((PER, 2, X, X), np.float32)
    for slot in range(PER):
        for e in range(8):
            table[slot, :, (X - 4 + e) % X, slot * 8 + e] = 1
    return table.reshape(PER // 2, 4 * X, X)


def halo_table():
    table = np.zeros((X, 4 * X), np.float32)
    for j in range(2):
        for side in range(2):
            e = 4 + j if side == 0 else 3 - j
            for slot, lane in ((1, 0), (2, T - 1)):
                table[slot * 8 + e, 2 * j * X + side * T + lane] = 1
            for slot, lane in ((0, 0), (1, 1), (2, T - 2), (3, T - 1)):
                table[slot * 8 + e, (2 * j + 1) * X + side * T + lane] = 1
    return table


def exact_dot(x, table):
    high, low = split(x)
    return dot(high, table) + dot(low, table)


def sine(n):
    rest = n & 1023
    folded = jnp.minimum(rest, 1024 - rest).astype(jnp.float32) * (math.pi / 1024)
    s = folded * folded
    p = jnp.float32(-2.5052108e-08)
    for c in (2.7557319e-06, -1.9841270e-04, 8.3333333e-03, -1.6666667e-01, 1.0):
        p = p * s + c
    p = p * folded
    return jnp.where(n < 1024, p, -p)


PARTS = (4 + LAG, 17, 31, SHARE + LAG + 2)


def edges_body(
    n_theta, n_ax,
    state, visc, rims, spread, place, halo, pick, stencil, coupling, block_map, plane_flags, cutoff,
    edges, sector, shared,
    q, nu, rim, fr, ft, axial, out, tabs, tabp, tabh, tabk, packed, packed_hal, rim_out, rim_in, edge, around, ax_out, ax_in,
    rad, sect, send_a, recv_a, send_b, recv_b, gh, gl, lhs, filt, res,
    in_sem, misc_sem, rim_send, rim_recv, halo_send, halo_recv, ax_send, ax_recv, a_send, a_recv, b_send, b_recv, out_sem,
):
    me = lax.axis_index("theta")
    my_ax = lax.axis_index("ax")
    nxt, prv = lax.rem(me + 1, n_theta), lax.rem(me + n_theta - 1, n_theta)
    right, left = lax.rem(my_ax + 1, n_ax), lax.rem(my_ax + n_ax - 1, n_ax)
    rs = R // n_theta

    def fetch(g):
        return pltpu.make_async_copy(
            state.at[:, pl.ds(g * PER, PER)],
            q.at[:, pl.ds(2 + g * PER, PER), pl.ds(TILE, R)],
            in_sem.at[g],
        )

    misc = [
        pltpu.make_async_copy(rims, rim, misc_sem.at[0]),
        pltpu.make_async_copy(visc, nu, misc_sem.at[1]),
        pltpu.make_async_copy(spread, tabs, misc_sem.at[2]),
        pltpu.make_async_copy(place, tabp, misc_sem.at[3]),
        pltpu.make_async_copy(halo, tabh, misc_sem.at[4]),
        pltpu.make_async_copy(pick, tabk, misc_sem.at[5]),
    ]
    for copy in misc[:2] + misc[5:]:
        copy.start()
    for g in range(GROUPS):
        fetch(g).start()
    for copy in misc[2:5]:
        copy.start()

    barrier = pltpu.get_barrier_semaphore()

    def greet(i, carry):
        pl.semaphore_signal(
            barrier, inc=1, device_id=(lax.rem(me + i, n_theta), my_ax), device_id_type=MESH
        )
        return carry

    lax.fori_loop(1, n_theta, greet, 0)
    for other in (left, right):
        pl.semaphore_signal(barrier, inc=1, device_id=(me, other), device_id_type=MESH)
    twice = 2 * cutoff[0] - 1

    def weights(b, carry):
        def some(i, carry):
            rows = pl.ds(pl.multiple_of(i * 16, 16), 16)
            down = lax.broadcasted_iota(jnp.int32, (16, 256), 0) + i * 16
            along = lax.broadcasted_iota(jnp.int32, (16, 256), 1)
            tau = (b * 256 + along - down) & 1023
            top = sine((twice * tau) & 2047)
            below = sine(jnp.maximum(tau, 1))
            ratio = jnp.where(tau == 0, twice.astype(jnp.float32), top / below)
            g = (ratio - 1.0) * (1.0 / 1024)
            high, low = split(g)
            gh[b, rows, :] = high
            gl[b, rows, :] = low
            return carry

        return lax.fori_loop(0, 16, some, carry)

    lax.fori_loop(0, 4, weights, 0)

    pl.semaphore_wait(barrier, n_theta + 1)

    def to_sector(i, cells, peer):
        return pltpu.make_async_remote_copy(
            src_ref=state.at[:, cells],
            dst_ref=q.at[:, pl.ds(i * (T + 2), 2), pl.ds(TILE, R)],
            send_sem=halo_send.at[i],
            recv_sem=halo_recv.at[i],
            device_id=(peer, my_ax),
            device_id_type=MESH,
        )

    halos = [to_sector(0, pl.ds(T - 2, 2), nxt), to_sector(1, pl.ds(0, 2), prv)]
    for copy in halos:
        copy.start()

    lane = lanes_of()
    slot_of = lane // 8

    def pack(load, slots):
        acc = None
        for slot in range(slots):
            turned = pltpu.roll(load(slot), (8 * slot + 4) % X, 1)
            if acc is None:
                acc = turned
            else:
                acc = jnp.where(slot_of[: turned.shape[0]] == slot, turned, acc)
        return acc

    for v in range(V + 1):
        packed[v, pl.ds(R, TILE), :] = jnp.zeros((TILE, GROUPS * X), jnp.float32)
    misc[0].wait()
    misc[1].wait()
    for g in range(GROUPS):
        cols = pl.ds(g * X, X)
        for v in range(V):
            packed[v, pl.ds(R, 4), cols] = pack(lambda t: rim[v, g * PER + t], PER)
    misc[5].wait()

    def group(g, carry):
        fetch(g).wait()
        cols = pl.ds(pl.multiple_of(g * X, X), X)
        tiles = [(v, k) for v in (3, 4, 5) for k in range(R // TILE)]
        total = None
        for two in range(PER // 2):
            tall = []
            for v in (0, 1, 2):
                wide = []
                for slot in (2 * two, 2 * two + 1):
                    wide += split(q[v, 2 + g * PER + slot, pl.ds(TILE, R), :])
                tall.append(jnp.concatenate(wide, axis=1))
            term = dot(jnp.concatenate(tall, axis=0), tabk[two])
            total = term if total is None else total + term
            for v, k in tiles[3 * two : 3 * two + 3]:
                rows, wide = pl.ds(k * TILE, TILE), pl.ds(k * TILE + TILE, TILE)
                if v < V:
                    packed[v, rows, cols] = pack(lambda t: q[v, 2 + g * PER + t, wide, :], PER)
                else:
                    packed[v, rows, cols] = pack(lambda t: nu[g * PER + t, rows, :], PER)
        for v in range(3):
            packed[v, pl.ds(0, R), cols] = total[v * R : (v + 1) * R]
        return carry

    lax.fori_loop(0, GROUPS, group, 0)
    for copy in misc[2:5]:
        copy.wait()

    high = R + TILE
    for some in (pl.ds(0, 3), pl.ds(3, 3)):
        got = exact_dot(packed[some].reshape(3 * high, GROUPS * X), tabs[...])
        for i in range(3):
            for j in range(4):
                edge[j, some.start + i] = got[i * high : (i + 1) * high, j * X : (j + 1) * X]

    first = lane < T

    def stage(k, carry):
        rows = pl.ds(pl.multiple_of(k * TILE, TILE), TILE)
        for v in range(V):
            near, far = edge[0, v, rows, :], edge[1, v, rows, :]
            ax_out[0, v, rows, :] = jnp.where(first, near, roll(far, T))
            ax_out[1, v, rows, :] = jnp.where(first, roll(near, T), far)
        return carry

    lax.fori_loop(0, R // TILE, stage, 0)

    def to_ax(i, peer):
        return pltpu.make_async_remote_copy(
            src_ref=ax_out.at[i],
            dst_ref=ax_in.at[i],
            send_sem=ax_send.at[i],
            recv_sem=ax_recv.at[i],
            device_id=(me, peer),
            device_id_type=MESH,
        )

    sides = [to_ax(0, left), to_ax(1, right)]
    has_left, has_right = my_ax > 0, my_ax < n_ax - 1

    @pl.when(has_left)
    def _():
        sides[0].start()

    @pl.when(has_right)
    def _():
        sides[1].start()

    @pl.when(jnp.logical_not(has_left))
    def _():
        ax_in[1] = ax_out[0]

    @pl.when(jnp.logical_not(has_right))
    def _():
        ax_in[0] = ax_out[0]

    block_of = lane // (2 * TILE)
    for v in range(V):
        for i, cols, start in ((0, (GROUPS - 1) * X, X - 2 * TILE), (1, 0, 0)):
            acc = None
            for k in range(R // TILE):
                own = packed[v, pl.ds(k * TILE, TILE), pl.ds(cols, X)]
                turned = roll(own, 2 * TILE * k - start)
                acc = turned if acc is None else jnp.where(block_of == k, turned, acc)
            rim_out[i, v] = acc

    def to_rim(i, peer):
        return pltpu.make_async_remote_copy(
            src_ref=rim_out.at[i],
            dst_ref=rim_in.at[i],
            send_sem=rim_send.at[i],
            recv_sem=rim_recv.at[i],
            device_id=(peer, my_ax),
            device_id_type=MESH,
        )

    ends = [to_rim(0, nxt), to_rim(1, prv)]
    for copy in ends:
        copy.start()

    to_hbm = []

    def radial(k, carry):
        rows = pl.ds(pl.multiple_of(k * TILE, TILE), TILE)
        wide = pl.ds(pl.multiple_of(k * TILE + TILE, TILE), TILE)
        for j in range(2):
            cell = [edge[j, v, rows, :] for v in range(V)]
            f = flux_r(cell, velocities(cell))
            for v in range(V):
                rad[j, v, wide, :] = f[v]
                rad[j, V + v, wide, :] = cell[v]
        return carry

    lax.fori_loop(0, R // TILE, radial, 0)
    for j in range(2):
        cell = [edge[j, v, pl.ds(R, TILE), :] for v in range(V)]
        f = flux_r(cell, velocities(cell))
        for v in range(V):
            for i, kept in ((v, f[v]), (V + v, cell[v])):
                rad[j, i, pl.ds(TILE - 2, 2), :] = kept[0:2]
                rad[j, i, pl.ds(TILE + R, 2), :] = kept[2:4]

    plane = plane_maker(q, nu, rim, fr, ft, axial, out, stencil)

    def planes(part):
        low, high = PARTS[part], PARTS[part + 1]

        def step(s, carry):
            plane(s)
            return carry

        lax.fori_loop(low, high, step, 0)
        t0, t1 = (2 if part == 0 else low - 2 - LAG), high - 2 - LAG
        copy = pltpu.make_async_copy(
            out.at[:, pl.ds(t0, t1 - t0)], shared.at[:, pl.ds(t0, t1 - t0)], out_sem.at[2 + part]
        )
        copy.start()
        to_hbm.append(copy)

    for s in range(2, 4 + LAG):
        plane(s, True, False, axial_before=s > 2)
    planes(0)

    for copy in ends:
        copy.wait_recv()
    for v in range(V):
        for k in range(R // TILE):
            before = roll(rim_in[0, v], -2 * TILE * k)
            after = roll(rim_in[1, v], 2 * TILE - 2 * TILE * k)
            packed_hal[v, pl.ds(k * TILE, TILE), :] = jnp.where(block_of == 0, before, after)

    def unpack_halo(v, carry):
        got = exact_dot(packed_hal[v], tabh[...])
        for i in range(4):
            around[i, v] = got[:, i * X : (i + 1) * X]
        return carry

    lax.fori_loop(0, V, unpack_halo, 0)

    @pl.when(has_right)
    def _():
        sides[0].wait_recv()

    @pl.when(has_left)
    def _():
        sides[1].wait_recv()

    sign = jnp.where(first, 1.0, -1.0).astype(jnp.float32)
    inside = jnp.where(first, has_left.astype(jnp.int32), has_right.astype(jnp.int32)) == 1
    at = lane & (T - 1)

    def section(k, carry):
        rows = pl.ds(pl.multiple_of(k * TILE, TILE), TILE)
        low = pl.multiple_of(k * TILE, TILE)
        cells, fluxes = {}, {}
        for j in range(-2, 4):
            if j >= 0:
                cell = [edge[j, v, rows, :] for v in range(V)]
            else:
                cell = []
                for v in range(V):
                    a, b = ax_in[1, v, rows, :], ax_in[0, v, rows, :]
                    if j == -1:
                        cell.append(jnp.where(first, a, roll(b, T)))
                    else:
                        cell.append(jnp.where(first, roll(a, T), b))
            vel = velocities(cell)
            f = flux_x(cell, vel)
            if j < 0:
                f = [jnp.where(inside, x, 0.0) for x in f]
                cell = [jnp.where(inside, x, 0.0) for x in cell]
            cells[j], fluxes[j] = cell, f
        for j in range(2):
            cell = cells[j]
            f = flux_t(cell, velocities(cell))
            halo_cell = [[around[2 * j + i, v, rows, :] for v in range(V)] for i in range(2)]
            halo_flux = [flux_t(c, velocities(c)) for c in halo_cell]
            n = edge[j, V, rows, :]
            n12 = 12.0 * n
            kq = 60.0 - 72.0 * n
            for v in range(V):

                def step(o, own, near, far):
                    ends = (at >= T - o) if o > 0 else (at < -o)
                    return jnp.where(ends, near if abs(o) == 1 else far, roll(own, -o))

                def cir(o):
                    return step(o, f[v], halo_flux[0][v], halo_flux[1][v])

                def cir_cell(o):
                    return step(o, cell[v], halo_cell[0][v], halo_cell[1][v])

                def r_at(i, o):
                    return rad[j, i, pl.ds(low + TILE + o, TILE), :]

                axial = 8.0 * (fluxes[j + 1][v] - fluxes[j - 1][v]) - (
                    fluxes[j + 2][v] - fluxes[j - 2][v]
                )
                near = (r_at(v, 1) - r_at(v, -1)) + (cir(1) - cir(-1))
                far = (r_at(v, 2) - r_at(v, -2)) + (cir(2) - cir(-2))
                side = (
                    (cells[j + 1][v] + cells[j - 1][v])
                    + (r_at(V + v, 1) + r_at(V + v, -1))
                    + (cir_cell(1) + cir_cell(-1))
                )
                sect[j, v, rows, :] = UNIT * (
                    kq * cell[v] + n12 * side - sign * axial - 8.0 * near + far
                )
        return carry

    lax.fori_loop(0, R // TILE, section, 0)

    for d in range(n_theta):
        send_a[d, pl.ds(V * rs, ROWS - V * rs), :] = jnp.zeros((ROWS - V * rs, X), jnp.float32)
        for v in range(V):
            send_a[d, pl.ds(v * rs, rs), :] = sect[0, v, pl.ds(d * rs, rs), :]

    def block_copy(src, dst, sems, i):
        peer = lax.rem(me + i, n_theta)
        return pltpu.make_async_remote_copy(
            src_ref=src.at[peer],
            dst_ref=dst.at[me],
            send_sem=sems[0].at[i],
            recv_sem=sems[1].at[i],
            device_id=(peer, my_ax),
            device_id_type=MESH,
        )

    def start_all(src, dst, sems):
        def go(i, carry):
            block_copy(src, dst, sems, i).start()
            return carry

        lax.fori_loop(1, n_theta, go, 0)

    def finish_all(src, dst, sems):
        def go(i, carry):
            block_copy(src, dst, sems, i).wait()
            return carry

        lax.fori_loop(1, n_theta, go, 0)

    start_all(send_a, recv_a, (a_send, a_recv))
    recv_a[me] = send_a[me]
    planes(1)
    finish_all(send_a, recv_a, (a_send, a_recv))

    wide_first = lanes_of(ROWS) < T
    for s in range(n_theta // 2):
        a, b = recv_a[2 * s], recv_a[2 * s + 1]
        cols = pl.ds(s * X, X)
        both = [jnp.where(wide_first, a, roll(b, T)), jnp.where(wide_first, roll(a, T), b)]
        for i in range(2):
            high, low = split(both[i])
            lhs[pl.ds(i * ROWS, ROWS), cols] = high.astype(jnp.float32)
            lhs[pl.ds((2 + i) * ROWS, ROWS), cols] = low.astype(jnp.float32)

    blocks = n_theta * T // 256
    terms = [lhs[:, a * 256 : (a + 1) * 256].astype(jnp.bfloat16) for a in range(blocks)]
    for b in range(blocks):
        total = None
        for a in range(blocks):
            k = (b - a) % blocks
            wide = dot(terms[a], gh[k])
            term = (wide[: 2 * ROWS] + wide[2 * ROWS :]) + dot(terms[a][: 2 * ROWS], gl[k])
            total = term if total is None else total + term
        filt[:, b * 256 : (b + 1) * 256] = total

    for s in range(n_theta // 2):
        cols = pl.ds(s * X, X)
        a, b = filt[pl.ds(0, ROWS), cols], filt[pl.ds(ROWS, ROWS), cols]
        send_b[2 * s] = jnp.where(wide_first, a, roll(b, T))
        send_b[2 * s + 1] = jnp.where(wide_first, roll(a, T), b)

    start_all(send_b, recv_b, (b_send, b_recv))
    recv_b[me] = send_b[me]
    planes(2)
    for copy in halos:
        copy.wait_recv()
    plane(0, False, False, True, False)
    plane(1, False, False, True, False)
    for s in (2, 3):
        plane(s + LAG, False, True, False, False)
    to_hbm.append(
        pltpu.make_async_copy(q.at[:, pl.ds(T + 2, 2), pl.ds(TILE, R)], sector, out_sem.at[0])
    )
    to_hbm.append(
        pltpu.make_async_copy(out.at[:, pl.ds(0, 2)], shared.at[:, pl.ds(0, 2)], out_sem.at[5])
    )
    for copy in to_hbm[-2:]:
        copy.start()
    finish_all(send_b, recv_b, (b_send, b_recv))

    flag = plane_flags[block_map[my_ax]]
    on = jnp.where(lanes_of(rs) < T, lax.rem(flag, 2), lax.div(flag, 2)) == 1
    for d in range(n_theta):
        mode = [recv_b[d, pl.ds(v * rs, rs), :] for v in range(V)]
        for u in range(V):
            added = coupling[u, 0] * mode[0]
            for v in range(1, V):
                added += coupling[u, v] * mode[v]
            rows = pl.ds(d * rs, rs)
            own = sect[0, u, rows, :]
            sect[0, u, rows, :] = jnp.where(on, own + added, own)

    for v in range(V):
        both = jnp.concatenate([sect[0, v], sect[1, v]], axis=1)
        got = exact_dot(both, tabp[...])
        for g in range(GROUPS):
            res[g, v] = got[:, g * X : (g + 1) * X]
    to_hbm.append(pltpu.make_async_copy(res, edges, out_sem.at[1]))
    to_hbm[-1].start()
    for copy in halos + ends:
        copy.wait_send()

    @pl.when(has_left)
    def _():
        sides[0].wait_send()

    @pl.when(has_right)
    def _():
        sides[1].wait_send()

    for copy in to_hbm:
        copy.wait()


def edges_call(mesh, state, visc, rims, stencil, coupling, block_map, plane_flags, cutoff):
    n_theta, n_ax = mesh.shape["theta"], mesh.shape["ax"]
    any_space = pl.BlockSpec(memory_space=pl.ANY)
    smem = pl.BlockSpec(memory_space=pltpu.SMEM)
    f32, bf16 = jnp.float32, jnp.bfloat16
    tabs = spread_table(range(4))
    tables = [
        jnp.asarray(x, bf16) for x in (tabs, tabs[:, : 2 * X].T, halo_table(), pick_table())
    ]
    dma = pltpu.SemaphoreType.DMA
    return pl.pallas_call(
        functools.partial(edges_body, n_theta, n_ax),
        out_shape=(
            jax.ShapeDtypeStruct((GROUPS, V, R, X), f32),
            jax.ShapeDtypeStruct((V, 2, R, X), f32),
            jax.ShapeDtypeStruct((V, SHARE, R, X), f32),
        ),
        in_specs=[any_space] * 7 + [pl.BlockSpec(memory_space=pltpu.VMEM)] + [smem] * 4,
        out_specs=(any_space, any_space, any_space),
        scratch_shapes=[
            pltpu.VMEM((V, T + 4, PAD, X), f32),
            pltpu.VMEM((T, R, X), f32),
            pltpu.VMEM((V, T, 4, X), f32),
            pltpu.VMEM((V - 1, SHARE + LAG, PAD, X), f32),
            pltpu.VMEM((V - 1, SHARE + LAG + 2, R, X), f32),
            pltpu.VMEM((V, R, 2 * X), bf16),
            pltpu.VMEM((V, SHARE + LAG, R, X), f32),
            pltpu.VMEM((GROUPS * X, 4 * X), bf16),
            pltpu.VMEM((2 * X, GROUPS * X), bf16),
            pltpu.VMEM((X, 4 * X), bf16),
            pltpu.VMEM((PER // 2, 4 * X, X), bf16),
            pltpu.VMEM((V + 1, R + TILE, GROUPS * X), f32),
            pltpu.VMEM((V, R, X), f32),
            pltpu.VMEM((2, V, TILE, X), f32),
            pltpu.VMEM((2, V, TILE, X), f32),
            pltpu.VMEM((4, V + 1, R + TILE, X), f32),
            pltpu.VMEM((4, V, R, X), f32),
            pltpu.VMEM((2, V, R, X), f32),
            pltpu.VMEM((2, V, R, X), f32),
            pltpu.VMEM((2, 2 * V, PAD, X), f32),
            pltpu.VMEM((2, V, R, X), f32),
            pltpu.VMEM((n_theta, ROWS, X), f32),
            pltpu.VMEM((n_theta, ROWS, X), f32),
            pltpu.VMEM((n_theta, ROWS, X), f32),
            pltpu.VMEM((n_theta, ROWS, X), f32),
            pltpu.VMEM((4, 256, 256), bf16),
            pltpu.VMEM((4, 256, 256), bf16),
            pltpu.VMEM((4 * ROWS, n_theta * T), f32),
            pltpu.VMEM((2 * ROWS, n_theta * T), f32),
            pltpu.VMEM((GROUPS, V, R, X), f32),
            dma((GROUPS,)),
            dma((6,)),
            dma((2,)),
            dma((2,)),
            dma((2,)),
            dma((2,)),
            dma((2,)),
            dma((2,)),
            dma((n_theta,)),
            dma((n_theta,)),
            dma((n_theta,)),
            dma((n_theta,)),
            dma((6,)),
        ],
        compiler_params=pltpu.CompilerParams(
            collective_id=0, has_side_effects=True, vmem_limit_bytes=60 * 1024 * 1024
        ),
        cost_estimate=pl.CostEstimate(
            flops=400_000_000, bytes_accessed=14_000_000, transcendentals=0
        ),
    )(state, visc, rims, *tables, stencil, coupling, block_map, plane_flags, cutoff)


def solution(mesh):
    def local(state, viscosity, band_rims, coupling, block_map, plane_flags, mode_cutoff):
        stencil = jnp.asarray(stencil_table(), jnp.bfloat16)
        edges, sector, shared = edges_call(
            mesh,
            state,
            viscosity,
            band_rims,
            stencil,
            coupling,
            block_map,
            plane_flags,
            mode_cutoff,
        )
        return section_call(state, viscosity, band_rims, sector, edges, shared, stencil)

    in_specs = (
        P(None, "theta", None, "ax"),
        P("theta", None, "ax"),
        P(None, "theta", None, "ax"),
        P(),
        P(),
        P(),
        P(),
    )
    out_specs = P(None, "theta", None, "ax")
    return jax.shard_map(local, mesh=mesh, in_specs=in_specs, out_specs=out_specs, check_vma=False)
```

```python
import functools
import math

import jax
import jax.numpy as jnp
import numpy as np
from jax import lax
from jax.experimental import pallas as pl
from jax.experimental.pallas import tpu as pltpu
from jax.sharding import PartitionSpec as P

UNIT = 0.2 / 12.0
V = 5
T = 64
R = 64
X = 128
TILE = 8
PAD = R + 2 * TILE
GROUPS = 4
PER = 16
CHUNK = 8
SHARE = 48
LAG = 3
ROWS = 24
MESH = pl.DeviceIdType.MESH


def inverse_of(density):
    guess = pl.reciprocal(density, approx=True)
    return guess * (2.0 - density * guess)


def velocities(q):
    inv = inverse_of(q[0])
    u, v, w = q[1] * inv, q[2] * inv, q[3] * inv
    p = 0.4 * (q[4] - 0.5 * (q[1] * u + q[2] * v + q[3] * w))
    return u, v, w, p, q[4] + p


def flux_x(q, vel):
    u, v, w, p, h = vel
    return [q[1], q[1] * u + p, q[2] * u, q[3] * u, h * u]


def flux_r(q, vel):
    u, v, w, p, h = vel
    return [q[2], q[2] * u, q[2] * v + p, q[3] * v, h * v]


def flux_t(q, vel):
    u, v, w, p, h = vel
    return [q[3], q[3] * u, q[3] * v, q[3] * w + p, h * w]


def roll(x, shift):
    return pltpu.roll(x, shift % X, 1)


def split(x):
    high = x.astype(jnp.bfloat16)
    return high, (x - high.astype(jnp.float32)).astype(jnp.bfloat16)


def dot(a, b):
    return jnp.dot(a, b, preferred_element_type=jnp.float32)


def stencil_table():
    table = np.zeros((X, X), np.float32)
    for x in range(X):
        for o, c in ((1, -8), (-1, 8), (2, 1), (-2, -1)):
            table[(x + o) % X, x] = c
    return np.concatenate([table, table])


def lanes_of(rows=TILE):
    return lax.broadcasted_iota(jnp.int32, (rows, X), 1)


def plane_maker(q, nu, rim, fr, ft, axial, res, stencil, turn_of=None, insert=None):
    pair = 2 * TILE

    def plane(s, first=True, second=True, circum=False, axial_before=True):
        q_near = q.at[:, pl.ds(s - LAG - 2, LAG + 3)] if second else q.at[:, pl.ds(s, 1)]
        ft_near = ft.at[:, pl.ds(s - LAG - 2, LAG + 3)] if second else ft.at[:, pl.ds(s, 1)]
        own = LAG + 2 if second else 0
        t = s - 2
        if second and first:
            fr_near, res_near, nu_near = (
                fr.at[:, pl.ds(t - LAG, LAG + 1)],
                res.at[:, pl.ds(t - LAG, LAG + 1)],
                nu.at[pl.ds(t - LAG, LAG + 1)],
            )
            new = LAG
        else:
            at = t - LAG if second else t
            if first or second:
                fr_near, res_near, nu_near = (
                    fr.at[:, pl.ds(at, 1)],
                    res.at[:, pl.ds(at, 1)],
                    nu.at[pl.ds(at, 1)],
                )
            new = 0

        def rims_of():
            for v in range(V):
                q_near[v, own, pl.ds(TILE - 2, 2), :] = rim[v, t, pl.ds(0, 2), :]
                q_near[v, own, pl.ds(TILE + R, 2), :] = rim[v, t, pl.ds(2, 2), :]
            cell = [rim[v, t, :, :] for v in range(V)]
            f = flux_r(cell, velocities(cell))
            for v in range(1, V):
                fr_near[v - 1, new, pl.ds(TILE - 2, 2), :] = f[v][0:2]
                fr_near[v - 1, new, pl.ds(TILE + R, 2), :] = f[v][2:4]

        def first_part(k):
            rows = pl.ds(k * pair, pair)
            wide = pl.ds(TILE + k * pair, pair)
            cell = [q_near[v, own, wide, :] for v in range(V)]
            vel = velocities(cell)
            f = flux_t(cell, vel)
            for v in range(1, V):
                ft_near[v - 1, own, rows, :] = f[v]
            if not first:
                return
            f = flux_x(cell, vel)
            for v in range(V):
                high, low = split(f[v])
                axial[v, rows, pl.ds(0, X)] = high
                axial[v, rows, pl.ds(X, X)] = low
            f = flux_r(cell, vel)
            for v in range(1, V):
                fr_near[v - 1, new, wide, :] = f[v]
            n = nu_near[new, rows, :]
            n12 = 12.0 * n
            kq = 60.0 - 72.0 * n
            for v in range(V):
                side = roll(cell[v], -1) + roll(cell[v], 1)
                res_near[v, new, rows, :] = kq * cell[v] + n12 * side

        if second:
            turn = turn_of(t - LAG) if insert is not None else None

        def second_part(k, v):
            rows = pl.ds(k * TILE, TILE)
            base = TILE + k * TILE
            n12 = 12.0 * nu_near[0, rows, :]

            def rad(o):
                at = pl.ds(base + o, TILE)
                return q_near[2, 2, at, :] if v == 0 else fr_near[v - 1, 0, at, :]

            def cir(o):
                if v == 0:
                    return q_near[3, 2 + o, pl.ds(base, TILE), :]
                return ft_near[v - 1, 2 + o, rows, :]

            near = (rad(1) - rad(-1)) + (cir(1) - cir(-1))
            far = (rad(2) - rad(-2)) + (cir(2) - cir(-2))
            side = (
                q_near[v, 2, pl.ds(base + 1, TILE), :] + q_near[v, 2, pl.ds(base - 1, TILE), :]
            ) + (q_near[v, 3, pl.ds(base, TILE), :] + q_near[v, 1, pl.ds(base, TILE), :])
            got = UNIT * (res_near[v, 0, rows, :] + n12 * side - 8.0 * near + far)
            if insert is not None:
                got = insert(turn, v, rows, got)
            res_near[v, 0, rows, :] = got

        if axial_before:
            before = res.at[:, pl.ds(t - 1, 1)] if new == 0 else res_near.at[:, pl.ds(new - 1, 1)]
            if second and not first:
                before = res.at[:, pl.ds(t - 1, 1)]
            for v in range(V):
                along = dot(axial[v], stencil[...])
                for k in range(R // pair):
                    rows = pl.ds(k * pair, pair)
                    before[v, 0, rows, :] += along[k * pair : (k + 1) * pair]
        if first:
            rims_of()
        for k in range(R // pair):
            if first or circum:
                first_part(k)
            if second:
                for v in range(V):
                    second_part(2 * k, v)
                    second_part(2 * k + 1, v)

    return plane


def section_body(
    state, visc, rims, sector, edges, shared, stencil, out,
    q, nu, rim, edg, fr, ft, axial, res, done, in_sem, misc_sem, out_sem, done_in, done_out,
):
    rest = T - SHARE
    n_chunks = rest // CHUNK

    def fetch(c):
        t0 = c * CHUNK
        return (
            pltpu.make_async_copy(
                state.at[:, pl.ds(SHARE + t0, CHUNK)],
                q.at[:, pl.ds(t0 + 2, CHUNK), pl.ds(TILE, R)],
                in_sem.at[0, c],
            ),
            pltpu.make_async_copy(
                visc.at[pl.ds(SHARE + t0, CHUNK)], nu.at[pl.ds(t0, CHUNK)], in_sem.at[1, c]
            ),
        )

    head = CHUNK - 1 - LAG
    each = SHARE // (rest - CHUNK + head)
    portions = [(0, head * each)]
    portions += [((head + CHUNK * (c - 1)) * each, CHUNK * each) for c in range(1, n_chunks)]

    def fetch_part(t0, count, c):
        planes = pl.ds(t0, count)
        return pltpu.make_async_copy(shared.at[:, planes], done.at[:, planes], done_in.at[c])

    def send_part(t0, count, c):
        planes = pl.ds(t0, count)
        return pltpu.make_async_copy(done.at[:, planes], out.at[:, planes], done_out.at[c])

    inner = pl.ds(TILE, R)
    misc = [
        pltpu.make_async_copy(
            state.at[:, pl.ds(SHARE - 2, 2)], q.at[:, pl.ds(0, 2), inner], misc_sem.at[0]
        ),
        pltpu.make_async_copy(sector, q.at[:, pl.ds(rest + 2, 2), inner], misc_sem.at[1]),
        pltpu.make_async_copy(rims.at[:, pl.ds(SHARE, rest)], rim, misc_sem.at[2]),
        pltpu.make_async_copy(edges, edg, misc_sem.at[3]),
    ]
    misc[0].start()
    misc[2].start()
    for copy in fetch(0):
        copy.start()
    misc[3].start()
    fetch_part(*portions[0], 0).start()
    for c in range(1, n_chunks):
        for copy in fetch(c):
            copy.start()
        fetch_part(*portions[c], c).start()
    misc[1].start()

    lane = lanes_of()
    edge_lanes = (lane < 2) | (lane >= X - 2)

    def turn_of(t):
        return t // PER, lax.rem(2 * X - 4 - 8 * lax.rem(t, PER), X)

    def insert(turn, v, rows, got):
        edge = pltpu.roll(edg[turn[0], v, rows, :], turn[1], 1)
        return jnp.where(edge_lanes, edge, got)

    plane = plane_maker(
        q, nu, rim, fr, ft, axial, res, stencil, lambda t: turn_of(t + SHARE), insert
    )

    def finish(t):
        turn = turn_of(t)
        near = done.at[:, pl.ds(t, 1)]
        for v in range(V):
            for k in range(R // TILE):
                rows = pl.ds(k * TILE, TILE)
                near[v, 0, rows, :] = insert(turn, v, rows, near[v, 0, rows, :])

    def send(t0, count, c):
        return pltpu.make_async_copy(
            res.at[:, pl.ds(t0, count)], out.at[:, pl.ds(SHARE + t0, count)], out_sem.at[c]
        )

    misc[0].wait()
    plane(0, False, False, True, False)
    plane(1, False, False, True, False)
    misc[2].wait()
    for copy in fetch(0):
        copy.wait()
    for s in range(2, 2 + LAG):
        plane(s, True, False, axial_before=s > 2)
    misc[3].wait()
    plane(2 + LAG)

    def steps(low, count):
        def step(i, carry):
            plane(low + i)
            for j in range(each):
                finish((low + i - 3 - LAG) * each + j)
            return carry

        lax.fori_loop(0, count, step, 0)

    fetch_part(*portions[0], 0).wait()
    steps(3 + LAG, head)
    send(0, CHUNK - LAG, 0).start()
    send_part(*portions[0], 0).start()

    def chunk(c, carry):
        for copy in fetch(c):
            copy.wait()
        t0 = (head + CHUNK * (c - 1)) * each
        fetch_part(t0, CHUNK * each, c).wait()
        steps(c * CHUNK + 2, CHUNK)
        send(c * CHUNK - LAG, CHUNK, c).start()
        send_part(t0, CHUNK * each, c).start()
        return carry

    lax.fori_loop(1, n_chunks, chunk, 0)
    misc[1].wait()
    for i in range(LAG):
        plane(rest + 2 + i, False, True, i < 2, i < 1)
    send(rest - LAG, LAG, n_chunks).start()
    send(0, CHUNK - LAG, 0).wait()

    def drain(c, carry):
        send(c * CHUNK - LAG, CHUNK, c).wait()
        send_part((head + CHUNK * (c - 1)) * each, CHUNK * each, c).wait()
        return carry

    lax.fori_loop(1, n_chunks, drain, 0)
    send_part(*portions[0], 0).wait()
    send(rest - LAG, LAG, n_chunks).wait()


def section_call(state, visc, rims, sector, edges, shared, stencil):
    any_space = pl.BlockSpec(memory_space=pl.ANY)
    f32 = jnp.float32
    rest = T - SHARE
    dma = pltpu.SemaphoreType.DMA
    return pl.pallas_call(
        section_body,
        out_shape=jax.ShapeDtypeStruct((V, T, R, X), f32),
        in_specs=[any_space] * 6 + [pl.BlockSpec(memory_space=pltpu.VMEM)],
        out_specs=any_space,
        scratch_shapes=[
            pltpu.VMEM((V, rest + 5, PAD, X), f32),
            pltpu.VMEM((rest, R, X), f32),
            pltpu.VMEM((V, rest, 4, X), f32),
            pltpu.VMEM((GROUPS, V, R, X), f32),
            pltpu.VMEM((V - 1, rest, PAD, X), f32),
            pltpu.VMEM((V - 1, rest + 5, R, X), f32),
            pltpu.VMEM((V, R, 2 * X), jnp.bfloat16),
            pltpu.VMEM((V, rest, R, X), f32),
            pltpu.VMEM((V, SHARE, R, X), f32),
            dma((2, rest // CHUNK)),
            dma((4,)),
            dma((rest // CHUNK + 1,)),
            dma((rest // CHUNK,)),
            dma((rest // CHUNK,)),
        ],
        compiler_params=pltpu.CompilerParams(vmem_limit_bytes=60 * 1024 * 1024),
        cost_estimate=pl.CostEstimate(
            flops=150 * rest * R * X, bytes_accessed=24_000_000, transcendentals=rest * R * X
        ),
    )(state, visc, rims, sector, edges, shared, stencil)


def spread_table(columns):
    table = np.zeros((GROUPS * X, len(columns) * X), np.float32)
    for place, j in enumerate(columns):
        for t in range(T):
            group, slot = divmod(t, PER)
            for side in range(2):
                e = 4 + j if side == 0 else 3 - j
                table[group * X + slot * 8 + e, place * X + side * T + t] = 1
    return table


def pick_table():
    table = np.zeros((PER, 2, X, X), np.float32)
    for slot in range(PER):
        for e in range(8):
            table[slot, :, (X - 4 + e) % X, slot * 8 + e] = 1
    return table.reshape(PER // 2, 4 * X, X)


def halo_table():
    table = np.zeros((X, 4 * X), np.float32)
    for j in range(2):
        for side in range(2):
            e = 4 + j if side == 0 else 3 - j
            for slot, lane in ((1, 0), (2, T - 1)):
                table[slot * 8 + e, 2 * j * X + side * T + lane] = 1
            for slot, lane in ((0, 0), (1, 1), (2, T - 2), (3, T - 1)):
                table[slot * 8 + e, (2 * j + 1) * X + side * T + lane] = 1
    return table


def exact_dot(x, table):
    high, low = split(x)
    return dot(high, table) + dot(low, table)


def sine(n):
    rest = n & 1023
    folded = jnp.minimum(rest, 1024 - rest).astype(jnp.float32) * (math.pi / 1024)
    s = folded * folded
    p = jnp.float32(-2.5052108e-08)
    for c in (2.7557319e-06, -1.9841270e-04, 8.3333333e-03, -1.6666667e-01, 1.0):
        p = p * s + c
    p = p * folded
    return jnp.where(n < 1024, p, -p)


PARTS = (4 + LAG, 21, 37, SHARE + LAG + 2)


def edges_body(
    n_theta, n_ax,
    state, visc, rims, spread, place, halo, pick, stencil, coupling, block_map, plane_flags, cutoff,
    edges, sector, shared,
    q, nu, rim, fr, ft, axial, out, tabs, tabp, tabh, tabk, packed, packed_hal, rim_out, rim_in, edge, around, ax_out, ax_in,
    rad, sect, send_a, recv_a, send_b, recv_b, gh, gl, lhs, filt, res,
    in_sem, misc_sem, rim_send, rim_recv, halo_send, halo_recv, ax_send, ax_recv, a_send, a_recv, b_send, b_recv, out_sem,
):
    me = lax.axis_index("theta")
    my_ax = lax.axis_index("ax")
    nxt, prv = lax.rem(me + 1, n_theta), lax.rem(me + n_theta - 1, n_theta)
    right, left = lax.rem(my_ax + 1, n_ax), lax.rem(my_ax + n_ax - 1, n_ax)
    rs = R // n_theta

    def fetch(g):
        return pltpu.make_async_copy(
            state.at[:, pl.ds(g * PER, PER)],
            q.at[:, pl.ds(2 + g * PER, PER), pl.ds(TILE, R)],
            in_sem.at[g],
        )

    misc = [
        pltpu.make_async_copy(rims, rim, misc_sem.at[0]),
        pltpu.make_async_copy(visc, nu, misc_sem.at[1]),
        pltpu.make_async_copy(spread, tabs, misc_sem.at[2]),
        pltpu.make_async_copy(place, tabp, misc_sem.at[3]),
        pltpu.make_async_copy(halo, tabh, misc_sem.at[4]),
        pltpu.make_async_copy(pick, tabk, misc_sem.at[5]),
    ]
    for copy in misc[:2] + misc[5:]:
        copy.start()
    for g in range(GROUPS):
        fetch(g).start()
    for copy in misc[2:5]:
        copy.start()

    barrier = pltpu.get_barrier_semaphore()

    def greet(i, carry):
        pl.semaphore_signal(
            barrier, inc=1, device_id=(lax.rem(me + i, n_theta), my_ax), device_id_type=MESH
        )
        return carry

    lax.fori_loop(1, n_theta, greet, 0)
    for other in (left, right):
        pl.semaphore_signal(barrier, inc=1, device_id=(me, other), device_id_type=MESH)
    twice = 2 * cutoff[0] - 1

    def weights(b, carry):
        def some(i, carry):
            rows = pl.ds(pl.multiple_of(i * 16, 16), 16)
            down = lax.broadcasted_iota(jnp.int32, (16, 256), 0) + i * 16
            along = lax.broadcasted_iota(jnp.int32, (16, 256), 1)
            tau = (b * 256 + along - down) & 1023
            top = sine((twice * tau) & 2047)
            below = sine(jnp.maximum(tau, 1))
            ratio = jnp.where(tau == 0, twice.astype(jnp.float32), top / below)
            g = (ratio - 1.0) * (1.0 / 1024)
            high, low = split(g)
            gh[b, rows, :] = high
            gl[b, rows, :] = low
            return carry

        return lax.fori_loop(0, 16, some, carry)

    lax.fori_loop(0, 4, weights, 0)

    pl.semaphore_wait(barrier, n_theta + 1)

    def to_sector(i, cells, peer):
        return pltpu.make_async_remote_copy(
            src_ref=state.at[:, cells],
            dst_ref=q.at[:, pl.ds(i * (T + 2), 2), pl.ds(TILE, R)],
            send_sem=halo_send.at[i],
            recv_sem=halo_recv.at[i],
            device_id=(peer, my_ax),
            device_id_type=MESH,
        )

    halos = [to_sector(0, pl.ds(T - 2, 2), nxt), to_sector(1, pl.ds(0, 2), prv)]
    for copy in halos:
        copy.start()

    lane = lanes_of()
    slot_of = lane // 8

    def pack(load, slots):
        acc = None
        for slot in range(slots):
            turned = pltpu.roll(load(slot), (8 * slot + 4) % X, 1)
            if acc is None:
                acc = turned
            else:
                acc = jnp.where(slot_of[: turned.shape[0]] == slot, turned, acc)
        return acc

    for v in range(V + 1):
        packed[v, pl.ds(R, TILE), :] = jnp.zeros((TILE, GROUPS * X), jnp.float32)
    misc[0].wait()
    misc[1].wait()
    for g in range(GROUPS):
        cols = pl.ds(g * X, X)
        for v in range(V):
            packed[v, pl.ds(R, 4), cols] = pack(lambda t: rim[v, g * PER + t], PER)
    misc[5].wait()

    def group(g, carry):
        fetch(g).wait()
        cols = pl.ds(pl.multiple_of(g * X, X), X)
        tiles = [(v, k) for v in (3, 4, 5) for k in range(R // TILE)]
        total = None
        for two in range(PER // 2):
            tall = []
            for v in (0, 1, 2):
                wide = []
                for slot in (2 * two, 2 * two + 1):
                    wide += split(q[v, 2 + g * PER + slot, pl.ds(TILE, R), :])
                tall.append(jnp.concatenate(wide, axis=1))
            term = dot(jnp.concatenate(tall, axis=0), tabk[two])
            total = term if total is None else total + term
            for v, k in tiles[3 * two : 3 * two + 3]:
                rows, wide = pl.ds(k * TILE, TILE), pl.ds(k * TILE + TILE, TILE)
                if v < V:
                    packed[v, rows, cols] = pack(lambda t: q[v, 2 + g * PER + t, wide, :], PER)
                else:
                    packed[v, rows, cols] = pack(lambda t: nu[g * PER + t, rows, :], PER)
        for v in range(3):
            packed[v, pl.ds(0, R), cols] = total[v * R : (v + 1) * R]
        return carry

    lax.fori_loop(0, GROUPS, group, 0)
    for copy in misc[2:5]:
        copy.wait()

    high = R + TILE
    for some in (pl.ds(0, 3), pl.ds(3, 3)):
        got = exact_dot(packed[some].reshape(3 * high, GROUPS * X), tabs[...])
        for i in range(3):
            for j in range(4):
                edge[j, some.start + i] = got[i * high : (i + 1) * high, j * X : (j + 1) * X]

    first = lane < T

    def stage(k, carry):
        rows = pl.ds(pl.multiple_of(k * TILE, TILE), TILE)
        for v in range(V):
            near, far = edge[0, v, rows, :], edge[1, v, rows, :]
            ax_out[0, v, rows, :] = jnp.where(first, near, roll(far, T))
            ax_out[1, v, rows, :] = jnp.where(first, roll(near, T), far)
        return carry

    lax.fori_loop(0, R // TILE, stage, 0)

    def to_ax(i, peer):
        return pltpu.make_async_remote_copy(
            src_ref=ax_out.at[i],
            dst_ref=ax_in.at[i],
            send_sem=ax_send.at[i],
            recv_sem=ax_recv.at[i],
            device_id=(me, peer),
            device_id_type=MESH,
        )

    sides = [to_ax(0, left), to_ax(1, right)]
    has_left, has_right = my_ax > 0, my_ax < n_ax - 1

    @pl.when(has_left)
    def _():
        sides[0].start()

    @pl.when(has_right)
    def _():
        sides[1].start()

    @pl.when(jnp.logical_not(has_left))
    def _():
        ax_in[1] = ax_out[0]

    @pl.when(jnp.logical_not(has_right))
    def _():
        ax_in[0] = ax_out[0]

    block_of = lane // (2 * TILE)
    for v in range(V):
        for i, cols, start in ((0, (GROUPS - 1) * X, X - 2 * TILE), (1, 0, 0)):
            acc = None
            for k in range(R // TILE):
                own = packed[v, pl.ds(k * TILE, TILE), pl.ds(cols, X)]
                turned = roll(own, 2 * TILE * k - start)
                acc = turned if acc is None else jnp.where(block_of == k, turned, acc)
            rim_out[i, v] = acc

    def to_rim(i, peer):
        return pltpu.make_async_remote_copy(
            src_ref=rim_out.at[i],
            dst_ref=rim_in.at[i],
            send_sem=rim_send.at[i],
            recv_sem=rim_recv.at[i],
            device_id=(peer, my_ax),
            device_id_type=MESH,
        )

    ends = [to_rim(0, nxt), to_rim(1, prv)]
    for copy in ends:
        copy.start()

    to_hbm = []

    def radial(k, carry):
        rows = pl.ds(pl.multiple_of(k * TILE, TILE), TILE)
        wide = pl.ds(pl.multiple_of(k * TILE + TILE, TILE), TILE)
        for j in range(2):
            cell = [edge[j, v, rows, :] for v in range(V)]
            f = flux_r(cell, velocities(cell))
            for v in range(V):
                rad[j, v, wide, :] = f[v]
                rad[j, V + v, wide, :] = cell[v]
        return carry

    lax.fori_loop(0, R // TILE, radial, 0)
    for j in range(2):
        cell = [edge[j, v, pl.ds(R, TILE), :] for v in range(V)]
        f = flux_r(cell, velocities(cell))
        for v in range(V):
            for i, kept in ((v, f[v]), (V + v, cell[v])):
                rad[j, i, pl.ds(TILE - 2, 2), :] = kept[0:2]
                rad[j, i, pl.ds(TILE + R, 2), :] = kept[2:4]

    plane = plane_maker(q, nu, rim, fr, ft, axial, out, stencil)

    def planes(part):
        low, high = PARTS[part], PARTS[part + 1]

        def step(s, carry):
            plane(s)
            return carry

        lax.fori_loop(low, high, step, 0)
        t0, t1 = (2 if part == 0 else low - 2 - LAG), high - 2 - LAG
        copy = pltpu.make_async_copy(
            out.at[:, pl.ds(t0, t1 - t0)], shared.at[:, pl.ds(t0, t1 - t0)], out_sem.at[2 + part]
        )
        copy.start()
        to_hbm.append(copy)

    for s in range(2, 4 + LAG):
        plane(s, True, False, axial_before=s > 2)
    planes(0)

    for copy in ends:
        copy.wait_recv()
    for v in range(V):
        for k in range(R // TILE):
            before = roll(rim_in[0, v], -2 * TILE * k)
            after = roll(rim_in[1, v], 2 * TILE - 2 * TILE * k)
            packed_hal[v, pl.ds(k * TILE, TILE), :] = jnp.where(block_of == 0, before, after)

    def unpack_halo(v, carry):
        got = exact_dot(packed_hal[v], tabh[...])
        for i in range(4):
            around[i, v] = got[:, i * X : (i + 1) * X]
        return carry

    lax.fori_loop(0, V, unpack_halo, 0)

    @pl.when(has_right)
    def _():
        sides[0].wait_recv()

    @pl.when(has_left)
    def _():
        sides[1].wait_recv()

    sign = jnp.where(first, 1.0, -1.0).astype(jnp.float32)
    inside = jnp.where(first, has_left.astype(jnp.int32), has_right.astype(jnp.int32)) == 1
    at = lane & (T - 1)

    def section(k, carry):
        rows = pl.ds(pl.multiple_of(k * TILE, TILE), TILE)
        low = pl.multiple_of(k * TILE, TILE)
        cells, fluxes = {}, {}
        for j in range(-2, 4):
            if j >= 0:
                cell = [edge[j, v, rows, :] for v in range(V)]
            else:
                cell = []
                for v in range(V):
                    a, b = ax_in[1, v, rows, :], ax_in[0, v, rows, :]
                    if j == -1:
                        cell.append(jnp.where(first, a, roll(b, T)))
                    else:
                        cell.append(jnp.where(first, roll(a, T), b))
            vel = velocities(cell)
            f = flux_x(cell, vel)
            if j < 0:
                f = [jnp.where(inside, x, 0.0) for x in f]
                cell = [jnp.where(inside, x, 0.0) for x in cell]
            cells[j], fluxes[j] = cell, f
        for j in range(2):
            cell = cells[j]
            f = flux_t(cell, velocities(cell))
            halo_cell = [[around[2 * j + i, v, rows, :] for v in range(V)] for i in range(2)]
            halo_flux = [flux_t(c, velocities(c)) for c in halo_cell]
            n = edge[j, V, rows, :]
            n12 = 12.0 * n
            kq = 60.0 - 72.0 * n
            for v in range(V):

                def step(o, own, near, far):
                    ends = (at >= T - o) if o > 0 else (at < -o)
                    return jnp.where(ends, near if abs(o) == 1 else far, roll(own, -o))

                def cir(o):
                    return step(o, f[v], halo_flux[0][v], halo_flux[1][v])

                def cir_cell(o):
                    return step(o, cell[v], halo_cell[0][v], halo_cell[1][v])

                def r_at(i, o):
                    return rad[j, i, pl.ds(low + TILE + o, TILE), :]

                axial = 8.0 * (fluxes[j + 1][v] - fluxes[j - 1][v]) - (
                    fluxes[j + 2][v] - fluxes[j - 2][v]
                )
                near = (r_at(v, 1) - r_at(v, -1)) + (cir(1) - cir(-1))
                far = (r_at(v, 2) - r_at(v, -2)) + (cir(2) - cir(-2))
                side = (
                    (cells[j + 1][v] + cells[j - 1][v])
                    + (r_at(V + v, 1) + r_at(V + v, -1))
                    + (cir_cell(1) + cir_cell(-1))
                )
                sect[j, v, rows, :] = UNIT * (
                    kq * cell[v] + n12 * side - sign * axial - 8.0 * near + far
                )
        return carry

    lax.fori_loop(0, R // TILE, section, 0)

    for d in range(n_theta):
        send_a[d, pl.ds(V * rs, ROWS - V * rs), :] = jnp.zeros((ROWS - V * rs, X), jnp.float32)
        for v in range(V):
            send_a[d, pl.ds(v * rs, rs), :] = sect[0, v, pl.ds(d * rs, rs), :]

    def block_copy(src, dst, sems, i):
        peer = lax.rem(me + i, n_theta)
        return pltpu.make_async_remote_copy(
            src_ref=src.at[peer],
            dst_ref=dst.at[me],
            send_sem=sems[0].at[i],
            recv_sem=sems[1].at[i],
            device_id=(peer, my_ax),
            device_id_type=MESH,
        )

    def start_all(src, dst, sems):
        def go(i, carry):
            block_copy(src, dst, sems, i).start()
            return carry

        lax.fori_loop(1, n_theta, go, 0)

    def finish_all(src, dst, sems):
        def go(i, carry):
            block_copy(src, dst, sems, i).wait()
            return carry

        lax.fori_loop(1, n_theta, go, 0)

    start_all(send_a, recv_a, (a_send, a_recv))
    recv_a[me] = send_a[me]
    planes(1)
    finish_all(send_a, recv_a, (a_send, a_recv))

    wide_first = lanes_of(ROWS) < T
    for s in range(n_theta // 2):
        a, b = recv_a[2 * s], recv_a[2 * s + 1]
        cols = pl.ds(s * X, X)
        both = [jnp.where(wide_first, a, roll(b, T)), jnp.where(wide_first, roll(a, T), b)]
        for i in range(2):
            high, low = split(both[i])
            lhs[pl.ds(i * ROWS, ROWS), cols] = high.astype(jnp.float32)
            lhs[pl.ds((2 + i) * ROWS, ROWS), cols] = low.astype(jnp.float32)

    blocks = n_theta * T // 256
    terms = [lhs[:, a * 256 : (a + 1) * 256].astype(jnp.bfloat16) for a in range(blocks)]
    for b in range(blocks):
        total = None
        for a in range(blocks):
            k = (b - a) % blocks
            wide = dot(terms[a], gh[k])
            term = (wide[: 2 * ROWS] + wide[2 * ROWS :]) + dot(terms[a][: 2 * ROWS], gl[k])
            total = term if total is None else total + term
        filt[:, b * 256 : (b + 1) * 256] = total

    for s in range(n_theta // 2):
        cols = pl.ds(s * X, X)
        a, b = filt[pl.ds(0, ROWS), cols], filt[pl.ds(ROWS, ROWS), cols]
        send_b[2 * s] = jnp.where(wide_first, a, roll(b, T))
        send_b[2 * s + 1] = jnp.where(wide_first, roll(a, T), b)

    start_all(send_b, recv_b, (b_send, b_recv))
    recv_b[me] = send_b[me]
    planes(2)
    for copy in halos:
        copy.wait_recv()
    plane(0, False, False, True, False)
    plane(1, False, False, True, False)
    for s in (2, 3):
        plane(s + LAG, False, True, False, False)
    to_hbm.append(
        pltpu.make_async_copy(q.at[:, pl.ds(T + 2, 2), pl.ds(TILE, R)], sector, out_sem.at[0])
    )
    to_hbm.append(
        pltpu.make_async_copy(out.at[:, pl.ds(0, 2)], shared.at[:, pl.ds(0, 2)], out_sem.at[5])
    )
    for copy in to_hbm[-2:]:
        copy.start()
    finish_all(send_b, recv_b, (b_send, b_recv))

    flag = plane_flags[block_map[my_ax]]
    on = jnp.where(lanes_of(rs) < T, lax.rem(flag, 2), lax.div(flag, 2)) == 1
    for d in range(n_theta):
        mode = [recv_b[d, pl.ds(v * rs, rs), :] for v in range(V)]
        for u in range(V):
            added = coupling[u, 0] * mode[0]
            for v in range(1, V):
                added += coupling[u, v] * mode[v]
            rows = pl.ds(d * rs, rs)
            own = sect[0, u, rows, :]
            sect[0, u, rows, :] = jnp.where(on, own + added, own)

    for v in range(V):
        both = jnp.concatenate([sect[0, v], sect[1, v]], axis=1)
        got = exact_dot(both, tabp[...])
        for g in range(GROUPS):
            res[g, v] = got[:, g * X : (g + 1) * X]
    to_hbm.append(pltpu.make_async_copy(res, edges, out_sem.at[1]))
    to_hbm[-1].start()
    for copy in halos + ends:
        copy.wait_send()

    @pl.when(has_left)
    def _():
        sides[0].wait_send()

    @pl.when(has_right)
    def _():
        sides[1].wait_send()

    for copy in to_hbm:
        copy.wait()


def edges_call(mesh, state, visc, rims, stencil, coupling, block_map, plane_flags, cutoff):
    n_theta, n_ax = mesh.shape["theta"], mesh.shape["ax"]
    any_space = pl.BlockSpec(memory_space=pl.ANY)
    smem = pl.BlockSpec(memory_space=pltpu.SMEM)
    f32, bf16 = jnp.float32, jnp.bfloat16
    tabs = spread_table(range(4))
    tables = [
        jnp.asarray(x, bf16) for x in (tabs, tabs[:, : 2 * X].T, halo_table(), pick_table())
    ]
    dma = pltpu.SemaphoreType.DMA
    return pl.pallas_call(
        functools.partial(edges_body, n_theta, n_ax),
        out_shape=(
            jax.ShapeDtypeStruct((GROUPS, V, R, X), f32),
            jax.ShapeDtypeStruct((V, 2, R, X), f32),
            jax.ShapeDtypeStruct((V, SHARE, R, X), f32),
        ),
        in_specs=[any_space] * 7 + [pl.BlockSpec(memory_space=pltpu.VMEM)] + [smem] * 4,
        out_specs=(any_space, any_space, any_space),
        scratch_shapes=[
            pltpu.VMEM((V, T + 4, PAD, X), f32),
            pltpu.VMEM((T, R, X), f32),
            pltpu.VMEM((V, T, 4, X), f32),
            pltpu.VMEM((V - 1, SHARE + LAG, PAD, X), f32),
            pltpu.VMEM((V - 1, SHARE + LAG + 2, R, X), f32),
            pltpu.VMEM((V, R, 2 * X), bf16),
            pltpu.VMEM((V, SHARE + LAG, R, X), f32),
            pltpu.VMEM((GROUPS * X, 4 * X), bf16),
            pltpu.VMEM((2 * X, GROUPS * X), bf16),
            pltpu.VMEM((X, 4 * X), bf16),
            pltpu.VMEM((PER // 2, 4 * X, X), bf16),
            pltpu.VMEM((V + 1, R + TILE, GROUPS * X), f32),
            pltpu.VMEM((V, R, X), f32),
            pltpu.VMEM((2, V, TILE, X), f32),
            pltpu.VMEM((2, V, TILE, X), f32),
            pltpu.VMEM((4, V + 1, R + TILE, X), f32),
            pltpu.VMEM((4, V, R, X), f32),
            pltpu.VMEM((2, V, R, X), f32),
            pltpu.VMEM((2, V, R, X), f32),
            pltpu.VMEM((2, 2 * V, PAD, X), f32),
            pltpu.VMEM((2, V, R, X), f32),
            pltpu.VMEM((n_theta, ROWS, X), f32),
            pltpu.VMEM((n_theta, ROWS, X), f32),
            pltpu.VMEM((n_theta, ROWS, X), f32),
            pltpu.VMEM((n_theta, ROWS, X), f32),
            pltpu.VMEM((4, 256, 256), bf16),
            pltpu.VMEM((4, 256, 256), bf16),
            pltpu.VMEM((4 * ROWS, n_theta * T), f32),
            pltpu.VMEM((2 * ROWS, n_theta * T), f32),
            pltpu.VMEM((GROUPS, V, R, X), f32),
            dma((GROUPS,)),
            dma((6,)),
            dma((2,)),
            dma((2,)),
            dma((2,)),
            dma((2,)),
            dma((2,)),
            dma((2,)),
            dma((n_theta,)),
            dma((n_theta,)),
            dma((n_theta,)),
            dma((n_theta,)),
            dma((6,)),
        ],
        compiler_params=pltpu.CompilerParams(
            collective_id=0, has_side_effects=True, vmem_limit_bytes=60 * 1024 * 1024
        ),
        cost_estimate=pl.CostEstimate(
            flops=400_000_000, bytes_accessed=14_000_000, transcendentals=0
        ),
    )(state, visc, rims, *tables, stencil, coupling, block_map, plane_flags, cutoff)


def solution(mesh):
    def local(state, viscosity, band_rims, coupling, block_map, plane_flags, mode_cutoff):
        stencil = jnp.asarray(stencil_table(), jnp.bfloat16)
        edges, sector, shared = edges_call(
            mesh,
            state,
            viscosity,
            band_rims,
            stencil,
            coupling,
            block_map,
            plane_flags,
            mode_cutoff,
        )
        return section_call(state, viscosity, band_rims, sector, edges, shared, stencil)

    in_specs = (
        P(None, "theta", None, "ax"),
        P("theta", None, "ax"),
        P(None, "theta", None, "ax"),
        P(),
        P(),
        P(),
        P(),
    )
    out_specs = P(None, "theta", None, "ax")
    return jax.shard_map(local, mesh=mesh, in_specs=in_specs, out_specs=out_specs, check_vma=False)
```
